512 devices in a mesh: rows: 128 (over z, y, core), grp: 4 (over x).
Axes of the slice: x: 4, y: 8, z: 8, core: 2. Of those that a mesh axis runs over, the one named last changes fastest.
Arguments:
- slab: float32 [4, 65536, 256], P('grp', 'rows'), as said below
- buckets: int32 [4, 65536], P('grp', 'rows'), may hold values from 0 to 255
- signs: int32 [4, 65536], P('grp', 'rows'), may hold values from -1 to 1, as said below
- counts: int32 [4, 16384], P('grp', 'rows'), may hold values from 1 to 4
Outputs:
- sketch: float32 [4, 32768, 256], P('grp', 'rows')
- factor: float32 [256, 256], replicated
The draws below stay inside these ranges and needn't reach their ends.
Inputs may be any that keep to these rules, and one draw needn't show every extreme that they name: Rows of the slab have varied scales and correlated columns. `signs`: each entry is -1 or +1.
All inputs are finite; a program needn't handle non-finite values.
Results may differ from the reference program's by a relative error of at most 0.0003.
Values sent between devices are 32-bit elements; how exact they have to be, the bound alone decides.
A program may use at most 64 MiB of HBM per device.

```python
import jax
import jax.numpy as jnp
from jax import lax

D = 256
CAP = 4
BPO = 256
SLOTS = 65536
N_ROWS = 128
N_GRP = 4


def draw_slab(key, part):
    key = jax.random.fold_in(key, 11)
    keys = jax.random.split(key, 5)
    total = N_ROWS * N_ROWS * CAP
    noise = jax.random.normal(keys[0], (N_GRP, total, D), jnp.float32)
    row_scale = jnp.exp(jax.random.uniform(keys[1], (N_GRP, total, 1), jnp.float32, jnp.log(0.3), jnp.log(3.0)))
    common = jax.random.normal(keys[2], (N_GRP, total, 4), jnp.float32)
    loads = 0.5 * jax.random.normal(keys[3], (4, D), jnp.float32)
    column_scale = jnp.exp(jax.random.uniform(keys[4], (D,), jnp.float32, jnp.log(0.5), jnp.log(2.0)))
    position = (jnp.arange(N_GRP, dtype=jnp.float32)[:, None] * total + jnp.arange(total, dtype=jnp.float32)[None, :]) / float(N_GRP * total)
    rising = jnp.exp(jnp.log(3.0) * position)[:, :, None]
    mixed = noise
    for index in range(4):
        mixed = mixed + common[:, :, index:index + 1] * loads[index]
    return (row_scale * rising * mixed * column_scale).astype(jnp.float32)


def draw_signs(key, part):
    key = jax.random.fold_in(key, 23)
    bits = jax.random.randint(key, (N_GRP, N_ROWS * N_ROWS * CAP), 0, 2)
    return (2 * bits - 1).astype(jnp.int32)


def draw_counts(key, part):
    key = jax.random.fold_in(key, 37)
    keys = jax.random.split(key, 2)
    lowest = max(1, CAP // 4)
    table = jax.random.randint(keys[0], (N_GRP, N_ROWS, N_ROWS), lowest, CAP + 1)
    target = jax.random.randint(keys[1], (N_GRP, 1, 1), 0, N_ROWS)
    column = jnp.arange(N_ROWS, dtype=jnp.int32)[None, None, :]
    table = jnp.where(column == target, CAP, table)
    return table.reshape(N_GRP, N_ROWS * N_ROWS).astype(jnp.int32)


def set_ends(drawn, stream_key, low, top_value):
    shape = drawn.shape
    index_at = [jax.random.randint(jax.random.fold_in(stream_key, axis), (), 0, shape[axis]) for axis in range(len(shape))]
    drawn = drawn.at[tuple(index_at)].set(low)
    longest = shape.index(max(shape))
    index_at[longest] = (index_at[longest] + 1) % shape[longest]
    return drawn.at[tuple(index_at)].set(top_value)


def setup_inputs(seed: int = 0) -> dict:
    key_of = jax.random.split(jax.random.key(seed), 5)
    return {
        "slab": draw_slab(jax.random.fold_in(key_of[4], 71), 0),
        "buckets": set_ends(jax.random.randint(key_of[1], (N_GRP, SLOTS), 0, BPO), jax.random.fold_in(key_of[1], 1), 0, BPO - 1).astype(jnp.int32),
        "signs": draw_signs(jax.random.fold_in(key_of[4], 71), 0),
        "counts": draw_counts(jax.random.fold_in(key_of[4], 71), 0),
    }


def reference(slab, buckets, signs, counts):
    slot = jnp.arange(N_ROWS * N_ROWS * CAP, dtype=jnp.int32)
    pair = slot // CAP
    owner = pair % N_ROWS
    place = slot % CAP

    def one_group(items):
        rows_in, bucket_in, sign_in, count_in = items
        used = place < count_in[pair]
        weight = jnp.where(used, sign_in, 0).astype(jnp.float32)
        ids = (owner * BPO + bucket_in).astype(jnp.int32)
        return jax.ops.segment_sum(rows_in * weight[:, None], ids, num_segments=N_ROWS * BPO)
    sketch = lax.map(one_group, (slab, buckets, signs, counts))
    gram = jnp.zeros((D, D), jnp.float32)
    for group in range(N_GRP):
        block = sketch[group]
        gram = gram + jnp.dot(block.T.astype(jnp.float32), block.astype(jnp.float32), precision=lax.Precision.HIGHEST, preferred_element_type=jnp.float32)
    gram = gram / float(N_GRP * N_ROWS * N_ROWS * CAP)
    factor = jnp.linalg.cholesky(gram).T
    return (sketch, factor)
```

```python
import jax
import jax.numpy as jnp
from jax import lax
from jax.experimental import pallas as pl
from jax.experimental.pallas import tpu as pltpu
from jax.sharding import PartitionSpec as P

NZ = 8
NY = 8
NX = 4
BPO = 256
HALF = 128
F32 = jnp.float32
BF16 = jnp.bfloat16
MESH = pl.DeviceIdType.MESH
ORDER = (4, 3, 5, 2, 6, 1, 7)


def gram_kernel(
    slab, meta, sk_out, g_out,
    r1a, r1b, r2a, r2b, m1, m2, mt, gp, gc, gh, gz, acc, gy, part, gx, fin, gfull,
    loc_sem, s1a_s, s1a_r, s1b_s, s1b_r, s1m_s, s1m_r, s2a_s, s2a_r, s2b_s, s2b_r, s2m_s, s2m_r,
    c_s, c_r, z_s, z_r, y_s, y_r, x_s, x_r, yg_s, yg_r, zg_s, zg_r, cg_s, cg_r,
):
    r = lax.axis_index("rows")
    x = lax.axis_index("grp")
    z = r // 16
    y = (r // 2) % 8
    c = r % 2
    oc = 1 - c

    def dev(zz, yy, cc, xx):
        return ((zz * NY + yy) * 2 + cc, xx)

    barrier = pltpu.get_barrier_semaphore()
    peers = [dev(z, y, oc, x)]
    for d in range(1, 8):
        for dc in range(2):
            peers.append(dev((z + d) % NZ, y, (c + dc) % 2, x))
            peers.append(dev(z, (y + d) % NY, (c + dc) % 2, x))
    for d in range(1, 4):
        peers.append(dev(z, y, c, (x + d) % NX))
    for p in peers:
        pl.semaphore_signal(barrier, inc=1, device_id=p, device_id_type=MESH)

    sends = []

    def rcopy(src, dst, ss, rs, to):
        cp = pltpu.make_async_remote_copy(
            src_ref=src, dst_ref=dst, send_sem=ss, recv_sem=rs, device_id=to, device_id_type=MESH
        )
        cp.start()
        sends.append(cp)
        return cp

    def lcopy(src, dst, sem):
        cp = pltpu.make_async_copy(src, dst, sem)
        cp.start()
        return cp

    la = lcopy(slab.at[z, :, :, pl.ds(0, HALF)], r1a.at[z], loc_sem.at[0])
    lb = lcopy(slab.at[:, y, :, pl.ds(HALF, HALF)], r1b.at[y], loc_sem.at[1])
    lm = lcopy(meta.at[pl.ds(z, 1)], m1.at[pl.ds(z, 1)], loc_sem.at[2])
    pl.semaphore_wait(barrier, len(peers))

    in_m, in_a, in_b = [], [], []
    for d in ORDER:
        zt = (z + d) % NZ
        in_m.append(rcopy(meta.at[pl.ds(zt, 1)], m1.at[pl.ds(z, 1)], s1m_s.at[d], s1m_r.at[d], dev(zt, y, c, x)))
    for d in ORDER:
        zt = (z + d) % NZ
        yt = (y + d) % NY
        in_a.append(rcopy(slab.at[zt, :, :, pl.ds(0, HALF)], r1a.at[z], s1a_s.at[d], s1a_r.at[d], dev(zt, y, c, x)))
        in_b.append(rcopy(slab.at[:, yt, :, pl.ds(HALF, HALF)], r1b.at[y], s1b_s.at[d], s1b_r.at[d], dev(z, yt, c, x)))

    lm.wait()
    for cp in in_m:
        cp.wait_recv()
    arrive = []
    for d in ORDER + (0,):
        for dc in range(2):
            if d == 0 and dc == 0:
                continue
            to = dev(z, (y + d) % NY, (c + dc) % 2, x)
            arrive.append(rcopy(m1, m2.at[c, y], s2m_s.at[d * 2 + dc], s2m_r.at[d * 2 + dc], to))
    m2[c, y] = m1[...]

    la.wait()
    for cp in in_a:
        cp.wait_recv()
    for d in ORDER + (0,):
        for dc in range(2):
            if d == 0 and dc == 0:
                continue
            yt = (y + d) % NY
            ct = (c + dc) % 2
            arrive.append(rcopy(
                r1a.at[:, yt, pl.ds(ct * 4, 4), :], r2a.at[y, :, pl.ds(c * 4, 4), :],
                s2a_s.at[d * 2 + dc], s2a_r.at[d * 2 + dc], dev(z, yt, ct, x),
            ))
    l2a = lcopy(r1a.at[:, y, pl.ds(c * 4, 4), :], r2a.at[y, :, pl.ds(c * 4, 4), :], loc_sem.at[3])
    lb.wait()
    for cp in in_b:
        cp.wait_recv()
    for d in ORDER + (0,):
        for dc in range(2):
            if d == 0 and dc == 0:
                continue
            zt = (z + d) % NZ
            ct = (c + dc) % 2
            arrive.append(rcopy(
                r1b.at[:, zt, pl.ds(ct * 4, 4), :], r2b.at[:, z, pl.ds(c * 4, 4), :],
                s2b_s.at[d * 2 + dc], s2b_r.at[d * 2 + dc], dev(zt, y, ct, x),
            ))
    l2b = lcopy(r1b.at[:, z, pl.ds(c * 4, 4), :], r2b.at[:, z, pl.ds(c * 4, 4), :], loc_sem.at[4])

    n_m = 15
    for cp in arrive[:n_m]:
        cp.wait_recv()
    mt[...] = jnp.transpose(m2[...].reshape(128, 128))
    b4 = mt[pl.ds(y * 8 + c * 4, 4), :]
    w4 = mt[pl.ds(64 + y * 8 + c * 4, 4), :]
    row = lax.broadcasted_iota(jnp.int32, (BPO, 128), 0)
    onehot = jnp.concatenate(
        [jnp.where(row == b4[s:s + 1, :], w4[s:s + 1, :], 0).astype(F32) for s in range(4)], axis=1
    ).astype(BF16)

    for cp in arrive[n_m:]:
        cp.wait_recv()
    l2a.wait()
    l2b.wait()
    fa = r2a.reshape(512, 128)
    fb = r2b.reshape(512, 128)
    rows = jnp.concatenate(
        [
            jnp.concatenate([f[pl.ds(k * 4 + s, 64, stride=8), :] for s in range(4) for k in range(2)], axis=0)
            for f in (fa, fb)
        ],
        axis=1,
    )
    hi = rows.astype(BF16)
    rest = rows - hi.astype(F32)
    mid = rest.astype(BF16)
    low = (rest - mid.astype(F32)).astype(BF16)
    sketch = jnp.dot(onehot, low, preferred_element_type=F32)
    sketch = sketch + jnp.dot(onehot, mid, preferred_element_type=F32)
    sketch = sketch + jnp.dot(onehot, hi, preferred_element_type=F32)
    sk_out[...] = sketch

    def outer(a, b):
        return lax.dot_general(
            a, b, (((0,), (0,)), ((), ())), precision=lax.Precision.HIGHEST, preferred_element_type=F32
        )

    left = sketch[:, :HALF]
    right = sketch[:, HALF:]
    gp[pl.ds(0, 128), :] = outer(left, left)
    gp[pl.ds(128, 128), :] = outer(left, right)
    gp[pl.ds(256, 128), :] = outer(right, right)

    sib = dev(z, y, oc, x)
    rcopy(gp.at[pl.ds(oc * 192, 192)], gc, c_s, c_r, sib).wait_recv()
    gh[...] = gp[pl.ds(pl.multiple_of(c * 192, 8), 192), :] + gc[...]

    got = []
    for d in ORDER:
        zt = (z + d) % NZ
        got.append(rcopy(gh.at[pl.ds(zt * 24, 24)], gz.at[d], z_s.at[d], z_r.at[d], dev(zt, y, c, x)))
    total = gh[pl.ds(pl.multiple_of(z * 24, 8), 24), :]
    for d, cp in zip(ORDER, got):
        cp.wait_recv()
        total = total + gz[d]
    acc[...] = total

    got = []
    for d in ORDER:
        yt = (y + d) % NY
        got.append(rcopy(acc.at[pl.ds(yt * 3, 3)], gy.at[d, pl.ds(0, 3)], y_s.at[d], y_r.at[d], dev(z, yt, c, x)))
    total = acc[pl.ds(y * 3, 3), :]
    for d, cp in zip(ORDER, got):
        cp.wait_recv()
        total = total + gy[d, 0:3]
    part[0:3, :] = total

    got = []
    for d in (2, 1, 3):
        xt = (x + d) % NX
        got.append(rcopy(part.at[pl.ds(0, 3)], gx.at[x, pl.ds(0, 3)], x_s.at[d], x_r.at[d], dev(z, y, c, xt)))
    gx[x, 0:3] = total
    for cp in got:
        cp.wait_recv()
    total = (gx[0, 0:3] + gx[1, 0:3]) + (gx[2, 0:3] + gx[3, 0:3])
    fin[pl.ds(y * 3, 3), :] = total

    got = []
    for d in ORDER:
        yt = (y + d) % NY
        got.append(rcopy(fin.at[pl.ds(y * 3, 3)], fin.at[pl.ds(y * 3, 3)], yg_s.at[d], yg_r.at[d], dev(z, yt, c, x)))
    for cp in got:
        cp.wait_recv()

    def place(zz):
        return gfull.at[pl.ds(c * 192 + zz * 24, 24)]

    got = []
    for d in ORDER:
        zt = (z + d) % NZ
        got.append(rcopy(fin, place(z), zg_s.at[d], zg_r.at[d], dev(zt, y, c, x)))
    over = [rcopy(fin, place(z), cg_s.at[0], cg_r.at[0], sib)]
    gfull[pl.ds(pl.multiple_of(c * 192 + z * 24, 8), 24), :] = fin[...]
    for d, cp in reversed(list(zip(ORDER, got))):
        cp.wait_recv()
        piece = place((z - d) % NZ)
        over.append(rcopy(piece, piece, cg_s.at[d], cg_r.at[d], sib))
    for cp in over:
        cp.wait_recv()
    g_out[...] = gfull[...]
    for cp in sends:
        cp.wait_send()


def factor_block(groups, lanes, n_lane_tiles, k0, emit):
    groups = list(groups)
    n = len(groups)
    for p in range(n):
        base = p * 8
        cols = [
            [jnp.broadcast_to(g[:, base + j:base + j + 1], (8, 128)) for j in range(8)] for g in groups[p:]
        ]
        diag = [[jnp.broadcast_to(cols[0][j][i:i + 1, :], (8, 128)) for j in range(i + 1)] for i in range(8)]
        low = [[None] * 8 for _ in range(8)]
        inv = []
        for j in range(8):
            rj = lax.rsqrt(diag[j][j])
            inv.append(rj)
            for i in range(j + 1, 8):
                low[i][j] = diag[i][j] * rj
            for i in range(j + 1, 8):
                for jj in range(j + 1, i + 1):
                    diag[i][jj] = diag[i][jj] - low[i][j] * low[jj][j]
        lead = groups[p]
        width = lead.shape[1]
        out = []
        inv_w = [jnp.concatenate([v] * (width // 128), axis=1) for v in inv]
        low_w = [[None if v is None else jnp.concatenate([v] * (width // 128), axis=1) for v in lr] for lr in low]
        for j in range(8):
            row = jnp.broadcast_to(lead[j:j + 1, :], (8, width))
            for i in range(j):
                row = row - low_w[j][i] * out[i]
            out.append(row * inv_w[j])
        for j in range(8):
            emit(k0 + base + j, base + j, out[j][0:1, :])
        for g in range(p + 1, n):
            mult = []
            for j in range(8):
                v = cols[g - p][j]
                for i in range(j):
                    v = v - low[j][i] * mult[i]
                mult.append(v * inv[j])
            upd = groups[g]
            for j in range(8):
                mw = jnp.concatenate([mult[j]] * (width // 128), axis=1)
                upd = upd - mw * out[j]
            groups[g] = upd


def factor_kernel(scale, g_ref, sk_ref, f_out, sk_out, sem):
    cp = pltpu.make_async_copy(sk_ref, sk_out, sem)
    cp.start()
    lane2 = lax.broadcasted_iota(jnp.int32, (1, 256), 1)
    lane1 = lax.broadcasted_iota(jnp.int32, (1, 128), 1)

    def emit_top(at, lane, value):
        f_out[at:at + 1, :] = jnp.where(lane2 >= lane, value, 0.0)

    def emit_bottom(at, lane, value):
        f_out[at:at + 1, 128:256] = jnp.where(lane1 >= lane, value, 0.0)

    top = []
    for p in range(16):
        a = g_ref[p * 8:p * 8 + 8, :] * scale
        b = g_ref[128 + p * 8:128 + p * 8 + 8, :] * scale
        top.append(jnp.concatenate([a, b], axis=1))
    f_out[128:256, 0:128] = jnp.zeros((128, 128), F32)
    factor_block(top, None, 2, 0, emit_top)
    side = f_out[0:128, 128:256]
    rest = g_ref[256:384, :] * scale - lax.dot_general(
        side, side, (((0,), (0,)), ((), ())), precision=lax.Precision.HIGHEST, preferred_element_type=F32
    )
    factor_block([rest[p * 8:p * 8 + 8, :] for p in range(16)], None, 1, 128, emit_bottom)
    cp.wait()


def body(slab, buckets, signs, counts):
    owners = lax.axis_size("rows")
    capacity = slab.shape[1] // owners
    width = slab.shape[2]
    place = lax.broadcasted_iota(jnp.int32, (owners, capacity), 1)
    weight = jnp.where(place < counts.reshape(owners, 1), signs.reshape(owners, capacity), 0)
    meta = jnp.concatenate([buckets.reshape(NZ, 64), weight.reshape(NZ, 64)], axis=1)
    vm = pl.BlockSpec(memory_space=pltpu.VMEM)
    anyspace = pl.BlockSpec(memory_space=pl.ANY)
    dma = pltpu.SemaphoreType.DMA
    sketch, gram = pl.pallas_call(
        gram_kernel,
        out_shape=(jax.ShapeDtypeStruct((BPO, width), F32), jax.ShapeDtypeStruct((384, 128), F32)),
        in_specs=[anyspace, vm],
        out_specs=(vm, vm),
        scratch_shapes=[
            pltpu.VMEM((8, 8, 8, 128), F32),
            pltpu.VMEM((8, 8, 8, 128), F32),
            pltpu.VMEM((8, 8, 8, 128), F32),
            pltpu.VMEM((8, 8, 8, 128), F32),
            pltpu.VMEM((8, 128), jnp.int32),
            pltpu.VMEM((2, 8, 8, 128), jnp.int32),
            pltpu.VMEM((128, 128), jnp.int32),
            pltpu.VMEM((384, 128), F32),
            pltpu.VMEM((192, 128), F32),
            pltpu.VMEM((192, 128), F32),
            pltpu.VMEM((8, 24, 128), F32),
            pltpu.VMEM((24, 128), F32),
            pltpu.VMEM((8, 8, 128), F32),
            pltpu.VMEM((8, 128), F32),
            pltpu.VMEM((4, 8, 128), F32),
            pltpu.VMEM((24, 128), F32),
            pltpu.VMEM((384, 128), F32),
            dma((5,)),
            dma((8,)), dma((8,)), dma((8,)), dma((8,)), dma((8,)), dma((8,)),
            dma((16,)), dma((16,)), dma((16,)), dma((16,)), dma((16,)), dma((16,)),
            dma, dma, dma((8,)), dma((8,)), dma((8,)), dma((8,)), dma((4,)), dma((4,)),
            dma((8,)), dma((8,)), dma((8,)), dma((8,)), dma((8,)), dma((8,)),
        ],
        compiler_params=pltpu.CompilerParams(
            collective_id=0, has_side_effects=True, vmem_limit_bytes=32 * 1024 * 1024
        ),
    )(slab.reshape(8, 8, 8, width), meta)
    slots = float(lax.axis_size("grp") * owners * owners * capacity)
    factor, sketch = pl.pallas_call(
        lambda *refs: factor_kernel(1.0 / slots, *refs),
        out_shape=(jax.ShapeDtypeStruct((width, width), F32), jax.ShapeDtypeStruct((BPO, width), F32)),
        in_specs=[vm, anyspace],
        out_specs=(vm, anyspace),
        scratch_shapes=[pltpu.SemaphoreType.DMA],
        compiler_params=pltpu.CompilerParams(vmem_limit_bytes=32 * 1024 * 1024),
    )(gram, sketch)
    return (sketch.reshape(1, BPO, width), factor)


def solution(mesh):
    in_specs = (P("grp", "rows", None), P("grp", "rows"), P("grp", "rows"), P("grp", "rows"))
    out_specs = (P("grp", "rows", None), P())
    return jax.shard_map(body, mesh=mesh, in_specs=in_specs, out_specs=out_specs, check_vma=False)
```

```python
import jax
import jax.numpy as jnp
from jax import lax
from jax.experimental import pallas as pl
from jax.experimental.pallas import tpu as pltpu
from jax.sharding import PartitionSpec as P

NZ = 8
NY = 8
NX = 4
BPO = 256
HALF = 128
F32 = jnp.float32
BF16 = jnp.bfloat16
MESH = pl.DeviceIdType.MESH
ORDER = (4, 3, 5, 2, 6, 1, 7)


def gram_kernel(
    slab_hbm, buckets_hbm, signs_hbm, counts_hbm, sk_out, g_out,
    slab, buckets, signs, counts, sk, meta, r1a, r1b, r2a, r2b, m1, m2, mt, gp, gx, acc, gz, part, gy, fin, gfull,
    loc_sem, s1a_s, s1a_r, s1b_s, s1b_r, s1m_s, s1m_r, s2a_s, s2a_r, s2b_s, s2b_r, s2m_s, s2m_r,
    x_s, x_r, z_s, z_r, y_s, y_r, zg_s, zg_r, xg_s, xg_r,
):
    r = lax.axis_index("rows")
    x = lax.axis_index("grp")
    z = r // 16
    y = (r // 2) % 8
    c = r % 2

    def dev(zz, yy, cc, xx):
        return ((zz * NY + yy) * 2 + cc, xx)

    barrier = pltpu.get_barrier_semaphore()
    peers = [dev(z, y, 1 - c, x)]
    for d in range(1, 8):
        for dc in range(2):
            peers.append(dev((z + d) % NZ, y, (c + dc) % 2, x))
            peers.append(dev(z, (y + d) % NY, (c + dc) % 2, x))
    for d in range(1, 4):
        for dc in range(2):
            peers.append(dev(z, y, (c + dc) % 2, (x + d) % NX))
    for p in peers:
        pl.semaphore_signal(barrier, inc=1, device_id=p, device_id_type=MESH)

    sends = []

    def rcopy(src, dst, ss, rs, to):
        cp = pltpu.make_async_remote_copy(
            src_ref=src, dst_ref=dst, send_sem=ss, recv_sem=rs, device_id=to, device_id_type=MESH
        )
        cp.start()
        sends.append(cp)
        return cp

    def lcopy(src, dst, sem):
        cp = pltpu.make_async_copy(src, dst, sem)
        cp.start()
        return cp

    load = lcopy(slab_hbm, slab, loc_sem.at[2])
    small = [
        lcopy(counts_hbm, counts, loc_sem.at[5]),
        lcopy(signs_hbm, signs, loc_sem.at[6]),
        lcopy(buckets_hbm, buckets, loc_sem.at[7]),
    ]
    slot = lax.broadcasted_iota(jnp.int32, (HALF, 512), 1)
    pair = lax.broadcasted_iota(jnp.int32, (HALF, 512), 0)
    spread = jnp.where(slot // 4 == pair, 1.0, 0.0).astype(BF16)
    for cp in small:
        cp.wait()
    limit = jnp.dot(
        jnp.broadcast_to(counts[...], (8, HALF)).astype(F32).astype(BF16), spread, preferred_element_type=F32
    )[0:1, :]
    place = lax.broadcasted_iota(jnp.int32, (1, 512), 1) % 4
    weight = jnp.where(place.astype(F32) < limit, signs[...], 0)
    for t in range(NZ):
        meta[t:t + 1, 0:64] = buckets[0:1, t * 64:t * 64 + 64]
        meta[t:t + 1, 64:128] = weight[0:1, t * 64:t * 64 + 64]
    load.wait()
    la = lcopy(slab.at[z, :, :, pl.ds(0, HALF)], r1a.at[z], loc_sem.at[0])
    lb = lcopy(slab.at[:, y, :, pl.ds(HALF, HALF)], r1b.at[y], loc_sem.at[1])
    m1[pl.ds(z, 1), :] = meta[pl.ds(z, 1), :]
    pl.semaphore_wait(barrier, len(peers))

    in_m, in_a, in_b = [], [], []
    for d in ORDER:
        zt = (z + d) % NZ
        in_m.append(rcopy(meta.at[pl.ds(zt, 1)], m1.at[pl.ds(z, 1)], s1m_s.at[d], s1m_r.at[d], dev(zt, y, c, x)))
    for d in ORDER:
        zt = (z + d) % NZ
        yt = (y + d) % NY
        in_a.append(rcopy(slab.at[zt, :, :, pl.ds(0, HALF)], r1a.at[z], s1a_s.at[d], s1a_r.at[d], dev(zt, y, c, x)))
        in_b.append(rcopy(slab.at[:, yt, :, pl.ds(HALF, HALF)], r1b.at[y], s1b_s.at[d], s1b_r.at[d], dev(z, yt, c, x)))

    for cp in in_m:
        cp.wait_recv()
    arrive = []
    for d in ORDER + (0,):
        for dc in range(2):
            if d == 0 and dc == 0:
                continue
            to = dev(z, (y + d) % NY, (c + dc) % 2, x)
            arrive.append(rcopy(m1, m2.at[c, y], s2m_s.at[d * 2 + dc], s2m_r.at[d * 2 + dc], to))
    m2[c, y] = m1[...]

    la.wait()
    for cp in in_a:
        cp.wait_recv()
    for d in ORDER + (0,):
        for dc in range(2):
            if d == 0 and dc == 0:
                continue
            yt = (y + d) % NY
            ct = (c + dc) % 2
            arrive.append(rcopy(
                r1a.at[:, yt, pl.ds(ct * 4, 4), :], r2a.at[y, :, pl.ds(c * 4, 4), :],
                s2a_s.at[d * 2 + dc], s2a_r.at[d * 2 + dc], dev(z, yt, ct, x),
            ))
    l2a = lcopy(r1a.at[:, y, pl.ds(c * 4, 4), :], r2a.at[y, :, pl.ds(c * 4, 4), :], loc_sem.at[3])
    lb.wait()
    for cp in in_b:
        cp.wait_recv()
    for d in ORDER + (0,):
        for dc in range(2):
            if d == 0 and dc == 0:
                continue
            zt = (z + d) % NZ
            ct = (c + dc) % 2
            arrive.append(rcopy(
                r1b.at[:, zt, pl.ds(ct * 4, 4), :], r2b.at[:, z, pl.ds(c * 4, 4), :],
                s2b_s.at[d * 2 + dc], s2b_r.at[d * 2 + dc], dev(zt, y, ct, x),
            ))
    l2b = lcopy(r1b.at[:, z, pl.ds(c * 4, 4), :], r2b.at[:, z, pl.ds(c * 4, 4), :], loc_sem.at[4])

    n_m = 15
    for cp in arrive[:n_m]:
        cp.wait_recv()
    mt[...] = jnp.transpose(m2[...].reshape(128, 128))
    b4 = mt[pl.ds(y * 8 + c * 4, 4), :]
    w4 = mt[pl.ds(64 + y * 8 + c * 4, 4), :]
    row = lax.broadcasted_iota(jnp.int32, (BPO, 128), 0)
    onehot = jnp.concatenate(
        [jnp.where(row == b4[s:s + 1, :], w4[s:s + 1, :], 0).astype(F32) for s in range(4)], axis=1
    ).astype(BF16)

    for cp in arrive[n_m:]:
        cp.wait_recv()
    l2a.wait()
    l2b.wait()
    fa = r2a.reshape(512, 128)
    fb = r2b.reshape(512, 128)
    rows = jnp.concatenate(
        [
            jnp.concatenate([f[pl.ds(k * 4 + s, 64, stride=8), :] for s in range(4) for k in range(2)], axis=0)
            for f in (fa, fb)
        ],
        axis=1,
    )
    hi = rows.astype(BF16)
    rest = rows - hi.astype(F32)
    mid = rest.astype(BF16)
    low = (rest - mid.astype(F32)).astype(BF16)
    sketch = jnp.dot(onehot, low, preferred_element_type=F32)
    sketch = sketch + jnp.dot(onehot, mid, preferred_element_type=F32)
    sketch = sketch + jnp.dot(onehot, hi, preferred_element_type=F32)
    sk[...] = sketch
    save = lcopy(sk, sk_out, loc_sem.at[8])

    def outer(a, b):
        return lax.dot_general(
            a, b, (((0,), (0,)), ((), ())), precision=lax.Precision.HIGHEST, preferred_element_type=F32
        )

    left = sketch[:, :HALF]
    right = sketch[:, HALF:]
    gp[pl.ds(0, 128), :] = outer(left, left)
    gp[pl.ds(128, 128), :] = outer(left, right)
    gp[pl.ds(256, 128), :] = outer(right, right)

    e = x * 2 + c
    near = [(d, dc) for d in (2, 1, 3, 0) for dc in range(2) if d or dc]
    got = []
    for d, dc in near:
        xt, ct = (x + d) % NX, (c + dc) % 2
        at = pl.ds((xt * 2 + ct) * 48, 48)
        got.append(rcopy(gp.at[at], gx.at[d * 2 + dc], x_s.at[d * 2 + dc], x_r.at[d * 2 + dc], dev(z, y, ct, xt)))
    total = gp[pl.ds(pl.multiple_of(e * 48, 8), 48), :]
    for (d, dc), cp in reversed(list(zip(near, got))):
        cp.wait_recv()
        total = total + gx[d * 2 + dc]
    acc[...] = total

    got = []
    for d in ORDER:
        zt = (z + d) % NZ
        got.append(rcopy(acc.at[pl.ds(zt * 6, 6)], gz.at[d, pl.ds(0, 6)], z_s.at[d], z_r.at[d], dev(zt, y, c, x)))
    total = acc[pl.ds(z * 6, 6), :]
    for d, cp in reversed(list(zip(ORDER, got))):
        cp.wait_recv()
        total = total + gz[d, 0:6]
    part[0:6, :] = total

    got = []
    for d in ORDER:
        yt = (y + d) % NY
        got.append(rcopy(part.at[pl.ds(0, 6)], gy.at[y, pl.ds(0, 6)], y_s.at[d], y_r.at[d], dev(z, yt, c, x)))
    gy[y, 0:6] = total
    for cp in got:
        cp.wait_recv()
    quad = [gy[2 * i, 0:6] + gy[2 * i + 1, 0:6] for i in range(4)]
    fin[pl.ds(z * 6, 6), :] = (quad[0] + quad[1]) + (quad[2] + quad[3])

    got = []
    mine = fin.at[pl.ds(z * 6, 6)]
    for d in ORDER:
        zt = (z + d) % NZ
        got.append(rcopy(mine, mine, zg_s.at[d], zg_r.at[d], dev(zt, y, c, x)))
    for cp in got:
        cp.wait_recv()

    got = []
    for d, dc in near:
        xt, ct = (x + d) % NX, (c + dc) % 2
        got.append(
            rcopy(fin, gfull.at[pl.ds(e * 48, 48)], xg_s.at[d * 2 + dc], xg_r.at[d * 2 + dc], dev(z, y, ct, xt))
        )
    gfull[pl.ds(pl.multiple_of(e * 48, 8), 48), :] = fin[...]
    for cp in got:
        cp.wait_recv()
    g_out[...] = gfull[...]
    save.wait()
    for cp in sends:
        cp.wait_send()


def splat(v):
    return jnp.broadcast_to(v, (8, HALF))


def recip(v):
    guess = pl.reciprocal(v, approx=True)
    guess = guess * (2.0 - v * guess)
    return guess * (2.0 - v * guess)


def factor_block(groups, k0, emit):
    n = len(groups)
    tiles = len(groups[0])
    for p in range(n):
        base = p * 8
        lead = groups[p]
        ahead = p + 1 < n
        column = [splat(lead[0][:, base + j:base + j + 1]) for j in range(8)]
        d = [[splat(column[j][i:i + 1, :]) for j in range(i + 1)] for i in range(8)]
        rows = [[splat(t[i:i + 1, :]) for t in lead] for i in range(8)]
        if ahead:
            nxt = list(groups[p + 1])
            side = [splat(nxt[0][:, base + j:base + j + 1]) for j in range(8)]
        final = []
        for b in range(0, 8, 2):
            p00, p10, p11 = d[b][b], d[b + 1][b], d[b + 1][b + 1]
            inv = recip(p00 * p11 - p10 * p10)
            x0, x1 = rows[b], rows[b + 1]
            if ahead:
                m0 = (p11 * side[b] - p10 * side[b + 1]) * inv
                m1 = (p00 * side[b + 1] - p10 * side[b]) * inv
                nxt = [t - (m0 * x0[k] + m1 * x1[k]) for k, t in enumerate(nxt)]
                for i in range(b + 2, 8):
                    side[i] = side[i] - (m0 * d[i][b] + m1 * d[i][b + 1])
            for i in range(b + 2, 8):
                n0 = p11 * d[i][b] - p10 * d[i][b + 1]
                n1 = p00 * d[i][b + 1] - p10 * d[i][b]
                for j in range(b + 2, i + 1):
                    d[i][j] = d[i][j] - (n0 * d[j][b] + n1 * d[j][b + 1]) * inv
                n0, n1 = n0 * inv, n1 * inv
                rows[i] = [t - (n0 * x0[k] + n1 * x1[k]) for k, t in enumerate(rows[i])]
            r0 = lax.rsqrt(p00)
            low = p10 * r0
            r1 = lax.rsqrt(p11 - low * low)
            first = [t * r0 for t in x0]
            final.append(first)
            final.append([(t - low * first[k]) * r1 for k, t in enumerate(x1)])
        for j in range(8):
            emit(k0 + base + j, base + j, [t[0:1, :] for t in final[j]])
        if ahead:
            groups[p + 1] = nxt
        if p + 2 < n:
            panel = jnp.concatenate([final[j][0][0:1, :] for j in range(8)], axis=0)
            turned = jnp.transpose(panel)
            for g in range(p + 2, n):
                mult = [splat(turned[g * 8:g * 8 + 8, j:j + 1]) for j in range(8)]
                for k in range(tiles):
                    terms = [mult[j] * final[j][k] for j in range(8)]
                    while len(terms) > 1:
                        terms = [terms[i] + terms[i + 1] for i in range(0, len(terms), 2)]
                    groups[g][k] = groups[g][k] - terms[0]


def factor_kernel(scale, g_ref, sk_ref, f_out, sk_out, sem):
    cp = pltpu.make_async_copy(sk_ref, sk_out, sem)
    cp.start()
    lane = lax.broadcasted_iota(jnp.int32, (8, HALF), 1)
    sub = lax.broadcasted_iota(jnp.int32, (8, HALF), 0)
    across, down = [], []
    for at in (0, 256):
        picked = [jnp.where(lane == sub + p * 8, g_ref[at + p * 8:at + p * 8 + 8, :], 0.0) for p in range(16)]
        down.append([lax.rsqrt(splat(jnp.sum(t, axis=1, keepdims=True))) for t in picked])
        while len(picked) > 1:
            picked = [picked[i] + picked[i + 1] for i in range(0, len(picked), 2)]
        across.append(splat(jnp.sum(picked[0], axis=0, keepdims=True)))
    scaled = [lax.rsqrt(v) for v in across]
    back = [jnp.sqrt(v * scale) for v in across]

    def emit(first):
        def put(at, diagonal, values):
            for k, v in enumerate(values):
                v = v * back[first + k][0:1, :]
                if k == 0:
                    v = jnp.where(lane[0:1, :] >= diagonal, v, 0.0)
                f_out[at:at + 1, (first + k) * HALF:(first + k + 1) * HALF] = v
                if keep is not None and k == 1:
                    keep.append(values[1])
        return put

    keep = []
    top = []
    for p in range(16):
        top.append([
            g_ref[p * 8:p * 8 + 8, :] * (down[0][p] * scaled[0]),
            g_ref[128 + p * 8:128 + p * 8 + 8, :] * (down[0][p] * scaled[1]),
        ])
    f_out[128:256, 0:128] = jnp.zeros((128, 128), F32)
    factor_block(top, 0, emit(0))
    corner = jnp.concatenate(keep, axis=0)
    keep = None
    less = lax.dot_general(
        corner, corner, (((0,), (0,)), ((), ())), precision=lax.Precision.HIGHEST, preferred_element_type=F32
    )
    bottom = []
    for p in range(16):
        at = 256 + p * 8
        bottom.append([g_ref[at:at + 8, :] * (down[1][p] * scaled[1]) - less[p * 8:p * 8 + 8, :]])
    factor_block(bottom, 128, emit(1))
    cp.wait()


def body(slab, buckets, signs, counts):
    owners = lax.axis_size("rows")
    capacity = slab.shape[1] // owners
    width = slab.shape[2]
    vm = pl.BlockSpec(memory_space=pltpu.VMEM)
    hbm = pl.BlockSpec(memory_space=pltpu.HBM)
    dma = pltpu.SemaphoreType.DMA
    sketch, gram = pl.pallas_call(
        gram_kernel,
        out_shape=(jax.ShapeDtypeStruct((BPO, width), F32), jax.ShapeDtypeStruct((384, 128), F32)),
        in_specs=[hbm] * 4,
        out_specs=(hbm, vm),
        scratch_shapes=[
            pltpu.VMEM((8, 8, 8, 256), F32),
            pltpu.VMEM((1, 512), jnp.int32),
            pltpu.VMEM((1, 512), jnp.int32),
            pltpu.VMEM((1, 128), jnp.int32),
            pltpu.VMEM((256, 256), F32),
            pltpu.VMEM((8, 128), jnp.int32),
            pltpu.VMEM((8, 8, 8, 128), F32),
            pltpu.VMEM((8, 8, 8, 128), F32),
            pltpu.VMEM((8, 8, 8, 128), F32),
            pltpu.VMEM((8, 8, 8, 128), F32),
            pltpu.VMEM((8, 128), jnp.int32),
            pltpu.VMEM((2, 8, 8, 128), jnp.int32),
            pltpu.VMEM((128, 128), jnp.int32),
            pltpu.VMEM((384, 128), F32),
            pltpu.VMEM((8, 48, 128), F32),
            pltpu.VMEM((48, 128), F32),
            pltpu.VMEM((8, 8, 128), F32),
            pltpu.VMEM((8, 128), F32),
            pltpu.VMEM((8, 8, 128), F32),
            pltpu.VMEM((48, 128), F32),
            pltpu.VMEM((384, 128), F32),
            dma((9,)),
            dma((8,)), dma((8,)), dma((8,)), dma((8,)), dma((8,)), dma((8,)),
            dma((16,)), dma((16,)), dma((16,)), dma((16,)), dma((16,)), dma((16,)),
            dma((8,)), dma((8,)), dma((8,)), dma((8,)), dma((8,)), dma((8,)),
            dma((8,)), dma((8,)), dma((8,)), dma((8,)),
        ],
        compiler_params=pltpu.CompilerParams(
            collective_id=0, has_side_effects=True, vmem_limit_bytes=60 * 1024 * 1024
        ),
    )(slab.reshape(8, 8, 8, width), buckets, signs, counts)
    slots = float(lax.axis_size("grp") * owners * owners * capacity)
    factor, sketch = pl.pallas_call(
        lambda *refs: factor_kernel(1.0 / slots, *refs),
        out_shape=(jax.ShapeDtypeStruct((width, width), F32), jax.ShapeDtypeStruct((BPO, width), F32)),
        in_specs=[vm, hbm],
        out_specs=(vm, hbm),
        scratch_shapes=[pltpu.SemaphoreType.DMA],
        compiler_params=pltpu.CompilerParams(vmem_limit_bytes=60 * 1024 * 1024),
    )(gram, sketch)
    return (sketch.reshape(1, BPO, width), factor)


def solution(mesh):
    in_specs = (P("grp", "rows", None), P("grp", "rows"), P("grp", "rows"), P("grp", "rows"))
    out_specs = (P("grp", "rows", None), P())
    return jax.shard_map(body, mesh=mesh, in_specs=in_specs, out_specs=out_specs, check_vma=False)
```

```python
import jax
import jax.numpy as jnp
from jax import lax
from jax.experimental import pallas as pl
from jax.experimental.pallas import tpu as pltpu
from jax.sharding import PartitionSpec as P

NZ = 8
NY = 8
NX = 4
BPO = 256
HALF = 128
F32 = jnp.float32
BF16 = jnp.bfloat16
MESH = pl.DeviceIdType.MESH
ORDER = (4, 3, 5, 2, 6, 1, 7)


def gram_kernel(
    slab_hbm, buckets_hbm, signs_hbm, counts_hbm, sk_out, g_out,
    ha, hb, buckets, signs, counts, sk, out1, r1a, r1b, r2a, r2b, mt, gp, gx, acc, gz, part, gy, fin, gfull,
    loc_sem, s1a_s, s1a_r, s1b_s, s1b_r, s2a_s, s2a_r, s2b_s, s2b_r,
    x_s, x_r, z_s, z_r, y_s, y_r, zg_s, zg_r, xg_s, xg_r,
):
    r = lax.axis_index("rows")
    x = lax.axis_index("grp")
    z = r // 16
    y = (r // 2) % 8
    c = r % 2

    def dev(zz, yy, cc, xx):
        return ((zz * NY + yy) * 2 + cc, xx)

    barrier = pltpu.get_barrier_semaphore()
    peers = [dev(z, y, 1 - c, x)]
    for d in range(1, 8):
        for dc in range(2):
            peers.append(dev((z + d) % NZ, y, (c + dc) % 2, x))
            peers.append(dev(z, (y + d) % NY, (c + dc) % 2, x))
    for d in range(1, 4):
        for dc in range(2):
            peers.append(dev(z, y, (c + dc) % 2, (x + d) % NX))
    for p in peers:
        pl.semaphore_signal(barrier, inc=1, device_id=p, device_id_type=MESH)

    sends = []

    def rcopy(src, dst, ss, rs, to):
        cp = pltpu.make_async_remote_copy(
            src_ref=src, dst_ref=dst, send_sem=ss, recv_sem=rs, device_id=to, device_id_type=MESH
        )
        cp.start()
        sends.append(cp)
        return cp

    def lcopy(src, dst, sem):
        cp = pltpu.make_async_copy(src, dst, sem)
        cp.start()
        return cp

    load = lcopy(slab_hbm.at[:, :, :, pl.ds(0, HALF)], ha, loc_sem.at[2])
    load_b = lcopy(slab_hbm.at[:, :, :, pl.ds(HALF, HALF)], hb, loc_sem.at[9])
    small = [
        lcopy(counts_hbm, counts, loc_sem.at[5]),
        lcopy(signs_hbm, signs, loc_sem.at[6]),
        lcopy(buckets_hbm, buckets, loc_sem.at[7]),
    ]
    for cp in small:
        cp.wait()

    def fold(values, each, first):
        count = values.shape[1]
        at = lax.broadcasted_iota(jnp.int32, (64, count), 1)
        pair = lax.broadcasted_iota(jnp.int32, (64, count), 0)
        mine = jnp.where(at // each == pair, values[...], 0).astype(F32).astype(BF16)
        src = lax.broadcasted_iota(jnp.int32, (count, HALF), 0)
        dst = lax.broadcasted_iota(jnp.int32, (count, HALF), 1)
        pick = jnp.where(src % each + first == dst, 1.0, 0.0).astype(BF16)
        return jnp.dot(mine, pick, preferred_element_type=F32)

    rows9 = out1.reshape(576, HALF)
    rows9[pl.ds(4, 64, stride=9), :] = fold(buckets, 8, 0) + fold(signs, 8, 8) + fold(counts, 2, 16)
    load.wait()
    flat = ha.reshape(512, HALF)
    for i in range(8):
        rows9[pl.ds(i + i // 4, 64, stride=9), :] = flat[pl.ds(i, 64, stride=8), :]
    load_b.wait()
    la = lcopy(out1.at[z], r1a.at[z], loc_sem.at[0])
    lb = lcopy(hb.at[:, y], r1b.at[y], loc_sem.at[1])
    pl.semaphore_wait(barrier, len(peers))

    in_a, in_b, arrive = [], [], []
    for d in ORDER:
        zt = (z + d) % NZ
        yt = (y + d) % NY
        in_a.append(rcopy(out1.at[zt], r1a.at[z], s1a_s.at[d], s1a_r.at[d], dev(zt, y, c, x)))
        in_b.append(rcopy(hb.at[:, yt], r1b.at[y], s1b_s.at[d], s1b_r.at[d], dev(z, yt, c, x)))

    la.wait()
    for cp in in_a:
        cp.wait_recv()
    for d in ORDER + (0,):
        for dc in range(2):
            if d == 0 and dc == 0:
                continue
            yt = (y + d) % NY
            ct = (c + dc) % 2
            arrive.append(rcopy(
                r1a.at[:, pl.ds(yt * 9 + ct * 4, 5), :], r2a.at[c, y, :, pl.ds(0, 5), :],
                s2a_s.at[d * 2 + dc], s2a_r.at[d * 2 + dc], dev(z, yt, ct, x),
            ))
    l2a = lcopy(r1a.at[:, pl.ds(y * 9 + c * 4, 5), :], r2a.at[c, y, :, pl.ds(0, 5), :], loc_sem.at[3])
    lb.wait()
    for cp in in_b:
        cp.wait_recv()
    for d in ORDER + (0,):
        for dc in range(2):
            if d == 0 and dc == 0:
                continue
            zt = (z + d) % NZ
            ct = (c + dc) % 2
            arrive.append(rcopy(
                r1b.at[:, zt, pl.ds(ct * 4, 4), :], r2b.at[:, z, pl.ds(c * 4, 4), :],
                s2b_s.at[d * 2 + dc], s2b_r.at[d * 2 + dc], dev(zt, y, ct, x),
            ))
    l2b = lcopy(r1b.at[:, z, pl.ds(c * 4, 4), :], r2b.at[:, z, pl.ds(c * 4, 4), :], loc_sem.at[4])

    l2a.wait()
    for cp in arrive[:15]:
        cp.wait_recv()
    fa = r2a.reshape(1024, HALF)
    fb = r2b.reshape(512, HALF)
    mt[...] = jnp.transpose(fa[pl.ds(4 - 4 * c, 128, stride=8), :])
    b4 = mt[pl.ds(c * 4, 4), :]
    s4 = mt[pl.ds(8 + c * 4, 4), :]
    used = mt[pl.ds(16 + c, 1), :]
    row = lax.broadcasted_iota(jnp.int32, (BPO, HALF), 0).astype(F32)
    onehot = jnp.concatenate(
        [jnp.where(row == b4[s:s + 1, :], jnp.where(used > s, s4[s:s + 1, :], 0.0), 0.0) for s in range(4)], axis=1
    ).astype(BF16)
    rows_a = jnp.concatenate([fa[pl.ds(s + c, 128, stride=8), :] for s in range(4)], axis=0)

    l2b.wait()
    for cp in arrive[15:]:
        cp.wait_recv()
    rows_b = jnp.concatenate(
        [fb[pl.ds(k * 4 + s, 64, stride=8), :] for s in range(4) for k in range(2)], axis=0
    )
    rows = jnp.concatenate([rows_a, rows_b], axis=1)
    hi = rows.astype(BF16)
    rest = rows - hi.astype(F32)
    mid = rest.astype(BF16)
    low = (rest - mid.astype(F32)).astype(BF16)
    sketch = jnp.dot(onehot, low, preferred_element_type=F32)
    sketch = sketch + jnp.dot(onehot, mid, preferred_element_type=F32)
    sketch = sketch + jnp.dot(onehot, hi, preferred_element_type=F32)
    sk[...] = sketch
    save = lcopy(sk, sk_out, loc_sem.at[8])

    turned = jnp.transpose(sketch)

    def pieces(v):
        first = v.astype(BF16)
        v = v - first.astype(F32)
        second = v.astype(BF16)
        return first, second, (v - second.astype(F32)).astype(BF16)

    ta, tb, tc = pieces(turned)
    sa, sb, sc = pieces(sketch)
    gram = jnp.zeros((BPO, BPO), F32)
    for left, right in ((tc, sa), (ta, sc), (tb, sb), (tb, sa), (ta, sb), (ta, sa)):
        gram = gram + jnp.dot(left, right, preferred_element_type=F32)
    gp[pl.ds(0, 128), :] = gram[:HALF, :HALF]
    gp[pl.ds(128, 128), :] = gram[:HALF, HALF:]
    gp[pl.ds(256, 128), :] = gram[HALF:, HALF:]

    e = x * 2 + c
    near = [(d, dc) for d in (2, 1, 3, 0) for dc in range(2) if d or dc]
    got = []
    for d, dc in near:
        xt, ct = (x + d) % NX, (c + dc) % 2
        at = pl.ds((xt * 2 + ct) * 48, 48)
        got.append(rcopy(gp.at[at], gx.at[d * 2 + dc], x_s.at[d * 2 + dc], x_r.at[d * 2 + dc], dev(z, y, ct, xt)))
    total = gp[pl.ds(pl.multiple_of(e * 48, 8), 48), :]
    for (d, dc), cp in reversed(list(zip(near, got))):
        cp.wait_recv()
        total = total + gx[d * 2 + dc]
    acc[...] = total

    got = []
    for d in ORDER:
        zt = (z + d) % NZ
        got.append(rcopy(acc.at[pl.ds(zt * 6, 6)], gz.at[d, pl.ds(0, 6)], z_s.at[d], z_r.at[d], dev(zt, y, c, x)))
    total = acc[pl.ds(z * 6, 6), :]
    for d, cp in reversed(list(zip(ORDER, got))):
        cp.wait_recv()
        total = total + gz[d, 0:6]
    part[0:6, :] = total

    got = []
    for d in ORDER:
        yt = (y + d) % NY
        got.append(rcopy(part.at[pl.ds(0, 6)], gy.at[y, pl.ds(0, 6)], y_s.at[d], y_r.at[d], dev(z, yt, c, x)))
    gy[y, 0:6] = total
    for cp in got:
        cp.wait_recv()
    quad = [gy[2 * i, 0:6] + gy[2 * i + 1, 0:6] for i in range(4)]
    fin[pl.ds(z * 6, 6), :] = (quad[0] + quad[1]) + (quad[2] + quad[3])

    got = []
    mine = fin.at[pl.ds(z * 6, 6)]
    for d in ORDER:
        zt = (z + d) % NZ
        got.append(rcopy(mine, mine, zg_s.at[d], zg_r.at[d], dev(zt, y, c, x)))
    for cp in got:
        cp.wait_recv()

    got = []
    for d, dc in near:
        xt, ct = (x + d) % NX, (c + dc) % 2
        got.append(
            rcopy(fin, gfull.at[pl.ds(e * 48, 48)], xg_s.at[d * 2 + dc], xg_r.at[d * 2 + dc], dev(z, y, ct, xt))
        )
    gfull[pl.ds(pl.multiple_of(e * 48, 8), 48), :] = fin[...]
    for cp in got:
        cp.wait_recv()
    g_out[...] = gfull[...]
    save.wait()
    for cp in sends:
        cp.wait_send()


def splat(v):
    return jnp.broadcast_to(v, (8, HALF))


def recip(v):
    guess = pl.reciprocal(v, approx=True)
    return guess * (2.0 - v * guess)


def factor_block(mats, k0, emit):
    tiles = len(mats)
    n = 16
    for p in range(n):
        base = p * 8
        ahead = p + 1 < n
        rows = [[m[pl.ds(base + i, 8, stride=0), :] for m in mats] for i in range(8)]
        d = [[splat(rows[i][0][:, base + j:base + j + 1]) for j in range(i + 1)] for i in range(8)]
        if ahead:
            nxt = [m[base + 8:base + 16, :] for m in mats]
            side = [splat(nxt[0][:, base + j:base + j + 1]) for j in range(8)]
        final = []
        for b in range(0, 8, 2):
            p00, p10, p11 = d[b][b], d[b + 1][b], d[b + 1][b + 1]
            inv = recip(p00 * p11 - p10 * p10)
            x0, x1 = rows[b], rows[b + 1]
            if ahead:
                n0 = p11 * side[b] - p10 * side[b + 1]
                n1 = p00 * side[b + 1] - p10 * side[b]
                nxt = [t - (n0 * x0[k] + n1 * x1[k]) * inv for k, t in enumerate(nxt)]
                if b < 6:
                    n0, n1 = n0 * inv, n1 * inv
                for i in range(b + 2, 8):
                    side[i] = side[i] - (n0 * d[i][b] + n1 * d[i][b + 1])
            for i in range(b + 2, 8):
                n0 = p11 * d[i][b] - p10 * d[i][b + 1]
                n1 = p00 * d[i][b + 1] - p10 * d[i][b]
                for j in range(b + 2, i + 1):
                    d[i][j] = d[i][j] - (n0 * d[j][b] + n1 * d[j][b + 1]) * inv
                n0, n1 = n0 * inv, n1 * inv
                rows[i] = [t - (n0 * x0[k] + n1 * x1[k]) for k, t in enumerate(rows[i])]
            r0 = lax.rsqrt(p00)
            low = p10 * r0
            r1 = lax.rsqrt(p11 - low * low)
            first = [t * r0 for t in x0]
            final.append(first)
            final.append([(t - low * first[k]) * r1 for k, t in enumerate(x1)])
        if ahead:
            for k, m in enumerate(mats):
                m[base + 8:base + 16, :] = nxt[k]
        for j in range(8):
            emit(k0 + base + j, base + j, [t[0:1, :] for t in final[j]])
        if p + 2 < n:
            panel = jnp.concatenate([final[j][0][0:1, :] for j in range(8)], axis=0)
            turned = jnp.transpose(panel)
            for g in range(p + 2, n):
                mult = [splat(turned[g * 8:g * 8 + 8, j:j + 1]) for j in range(8)]
                for k, m in enumerate(mats):
                    terms = [mult[j] * final[j][k] for j in range(8)]
                    while len(terms) > 1:
                        terms = [terms[i] + terms[i + 1] for i in range(0, len(terms), 2)]
                    m[g * 8:g * 8 + 8, :] = m[g * 8:g * 8 + 8, :] - terms[0]


def factor_kernel(scale, g_ref, sk_ref, f_out, sk_out, a0, a1, sem):
    cp = pltpu.make_async_copy(sk_ref, sk_out, sem)
    cp.start()
    lane = lax.broadcasted_iota(jnp.int32, (8, HALF), 1)
    sub = lax.broadcasted_iota(jnp.int32, (8, HALF), 0)
    across, down = [], []
    for at in (0, 256):
        picked = [jnp.where(lane == sub + p * 8, g_ref[at + p * 8:at + p * 8 + 8, :], 0.0) for p in range(16)]
        down.append([lax.rsqrt(splat(jnp.sum(t, axis=1, keepdims=True))) for t in picked])
        while len(picked) > 1:
            picked = [picked[i] + picked[i + 1] for i in range(0, len(picked), 2)]
        across.append(splat(jnp.sum(picked[0], axis=0, keepdims=True)))
    scaled = [lax.rsqrt(v) for v in across]
    back = [jnp.sqrt(v * scale) for v in across]

    def emit(first):
        def put(at, diagonal, values):
            for k, v in enumerate(values):
                v = v * back[first + k][0:1, :]
                if k == 0:
                    v = jnp.where(lane[0:1, :] >= diagonal, v, 0.0)
                f_out[at:at + 1, (first + k) * HALF:(first + k + 1) * HALF] = v
        return put

    for p in range(16):
        at = p * 8
        a0[at:at + 8, :] = g_ref[at:at + 8, :] * (down[0][p] * scaled[0])
        a1[at:at + 8, :] = g_ref[128 + at:128 + at + 8, :] * (down[0][p] * scaled[1])
    f_out[128:256, 0:128] = jnp.zeros((128, 128), F32)
    factor_block([a0, a1], 0, emit(0))
    corner = f_out[0:128, 128:256]
    less = lax.dot_general(
        corner, corner, (((0,), (0,)), ((), ())), precision=lax.Precision.HIGHEST, preferred_element_type=F32
    )
    for p in range(16):
        at = p * 8
        left = g_ref[256 + at:256 + at + 8, :] - less[at:at + 8, :] * (1.0 / scale)
        a0[at:at + 8, :] = left * (down[1][p] * scaled[1])
    factor_block([a0], 128, emit(1))
    cp.wait()


def body(slab, buckets, signs, counts):
    owners = lax.axis_size("rows")
    capacity = slab.shape[1] // owners
    width = slab.shape[2]
    vm = pl.BlockSpec(memory_space=pltpu.VMEM)
    hbm = pl.BlockSpec(memory_space=pltpu.HBM)
    dma = pltpu.SemaphoreType.DMA
    sketch, gram = pl.pallas_call(
        gram_kernel,
        out_shape=(jax.ShapeDtypeStruct((BPO, width), F32), jax.ShapeDtypeStruct((384, 128), F32)),
        in_specs=[hbm] * 4,
        out_specs=(hbm, vm),
        scratch_shapes=[
            pltpu.VMEM((8, 8, 8, 128), F32),
            pltpu.VMEM((8, 8, 8, 128), F32),
            pltpu.VMEM((1, 512), jnp.int32),
            pltpu.VMEM((1, 512), jnp.int32),
            pltpu.VMEM((1, 128), jnp.int32),
            pltpu.VMEM((256, 256), F32),
            pltpu.VMEM((8, 72, 128), F32),
            pltpu.VMEM((8, 72, 128), F32),
            pltpu.VMEM((8, 8, 8, 128), F32),
            pltpu.VMEM((2, 8, 8, 8, 128), F32),
            pltpu.VMEM((8, 8, 8, 128), F32),
            pltpu.VMEM((128, 128), F32),
            pltpu.VMEM((384, 128), F32),
            pltpu.VMEM((8, 48, 128), F32),
            pltpu.VMEM((48, 128), F32),
            pltpu.VMEM((8, 8, 128), F32),
            pltpu.VMEM((8, 128), F32),
            pltpu.VMEM((8, 8, 128), F32),
            pltpu.VMEM((48, 128), F32),
            pltpu.VMEM((384, 128), F32),
            dma((10,)),
            dma((8,)), dma((8,)), dma((8,)), dma((8,)),
            dma((16,)), dma((16,)), dma((16,)), dma((16,)),
            dma((8,)), dma((8,)), dma((8,)), dma((8,)), dma((8,)), dma((8,)),
            dma((8,)), dma((8,)), dma((8,)), dma((8,)),
        ],
        compiler_params=pltpu.CompilerParams(
            collective_id=0, has_side_effects=True, vmem_limit_bytes=60 * 1024 * 1024
        ),
    )(slab.reshape(8, 8, 8, width), buckets, signs, counts)
    slots = float(lax.axis_size("grp") * owners * owners * capacity)
    factor, sketch = pl.pallas_call(
        lambda *refs: factor_kernel(1.0 / slots, *refs),
        out_shape=(jax.ShapeDtypeStruct((width, width), F32), jax.ShapeDtypeStruct((BPO, width), F32)),
        in_specs=[vm, hbm],
        out_specs=(vm, hbm),
        scratch_shapes=[
            pltpu.VMEM((HALF, HALF), F32),
            pltpu.VMEM((HALF, HALF), F32),
            pltpu.SemaphoreType.DMA,
        ],
        compiler_params=pltpu.CompilerParams(vmem_limit_bytes=60 * 1024 * 1024),
    )(gram, sketch)
    return (sketch.reshape(1, BPO, width), factor)


def solution(mesh):
    in_specs = (P("grp", "rows", None), P("grp", "rows"), P("grp", "rows"), P("grp", "rows"))
    out_specs = (P("grp", "rows", None), P())
    return jax.shard_map(body, mesh=mesh, in_specs=in_specs, out_specs=out_specs, check_vma=False)
```

```python
import jax
import jax.numpy as jnp
from jax import lax
from jax.experimental import pallas as pl
from jax.experimental.pallas import tpu as pltpu
from jax.sharding import PartitionSpec as P

NZ = 8
NY = 8
NX = 4
BPO = 256
HALF = 128
F32 = jnp.float32
BF16 = jnp.bfloat16
MESH = pl.DeviceIdType.MESH
ORDER = (4, 3, 5, 2, 6, 1, 7)


def gram_kernel(
    slab_hbm, buckets_hbm, signs_hbm, counts_hbm, sk_out, g_out,
    slab, buckets, signs, counts, sk, meta, r1a, r1b, r2a, r2b, m1, m2, mt, gp, gx, acc, gz, part, gy, fin, gfull,
    loc_sem, s1a_s, s1a_r, s1b_s, s1b_r, s1m_s, s1m_r, s2a_s, s2a_r, s2b_s, s2b_r, s2m_s, s2m_r,
    x_s, x_r, z_s, z_r, y_s, y_r, zg_s, zg_r, xg_s, xg_r,
):
    r = lax.axis_index("rows")
    x = lax.axis_index("grp")
    z = r // 16
    y = (r // 2) % 8
    c = r % 2

    def dev(zz, yy, cc, xx):
        return ((zz * NY + yy) * 2 + cc, xx)

    barrier = pltpu.get_barrier_semaphore()
    peers = [dev(z, y, 1 - c, x)]
    for d in range(1, 8):
        for dc in range(2):
            peers.append(dev((z + d) % NZ, y, (c + dc) % 2, x))
            peers.append(dev(z, (y + d) % NY, (c + dc) % 2, x))
    for d in range(1, 4):
        for dc in range(2):
            peers.append(dev(z, y, (c + dc) % 2, (x + d) % NX))
    for p in peers:
        pl.semaphore_signal(barrier, inc=1, device_id=p, device_id_type=MESH)

    sends = []

    def rcopy(src, dst, ss, rs, to):
        cp = pltpu.make_async_remote_copy(
            src_ref=src, dst_ref=dst, send_sem=ss, recv_sem=rs, device_id=to, device_id_type=MESH
        )
        cp.start()
        sends.append(cp)
        return cp

    def lcopy(src, dst, sem):
        cp = pltpu.make_async_copy(src, dst, sem)
        cp.start()
        return cp

    load = lcopy(slab_hbm, slab, loc_sem.at[2])
    small = [
        lcopy(counts_hbm, counts, loc_sem.at[5]),
        lcopy(signs_hbm, signs, loc_sem.at[6]),
        lcopy(buckets_hbm, buckets, loc_sem.at[7]),
    ]
    slot = lax.broadcasted_iota(jnp.int32, (HALF, 512), 1)
    pair = lax.broadcasted_iota(jnp.int32, (HALF, 512), 0)
    spread = jnp.where(slot // 4 == pair, 1.0, 0.0).astype(BF16)
    for cp in small:
        cp.wait()
    limit = jnp.dot(
        jnp.broadcast_to(counts[...], (8, HALF)).astype(F32).astype(BF16), spread, preferred_element_type=F32
    )[0:1, :]
    place = lax.broadcasted_iota(jnp.int32, (1, 512), 1) % 4
    weight = jnp.where(place.astype(F32) < limit, signs[...], 0)
    for t in range(NZ):
        meta[t:t + 1, 0:64] = buckets[0:1, t * 64:t * 64 + 64]
        meta[t:t + 1, 64:128] = weight[0:1, t * 64:t * 64 + 64]
    load.wait()
    own = {}
    for q in range(2):
        yl, zl = (y + q) % 2, (z + q) % 2
        own[q] = (
            lcopy(slab.at[z // 2, z % 2, :, yl, :, pl.ds(0, HALF)], r1a.at[z, yl], loc_sem.at[9 + q]),
            lcopy(slab.at[:, zl, y // 2, y % 2, :, pl.ds(HALF, HALF)], r1b.at[y, zl], loc_sem.at[11 + q]),
        )
    m1[pl.ds(z, 1), :] = meta[pl.ds(z, 1), :]
    pl.semaphore_wait(barrier, len(peers))

    in_m = []
    for d in ORDER:
        zt = (z + d) % NZ
        in_m.append(rcopy(meta.at[pl.ds(zt, 1)], m1.at[pl.ds(z, 1)], s1m_s.at[d], s1m_r.at[d], dev(zt, y, c, x)))
    in_a, in_b = {0: [], 1: []}, {0: [], 1: []}
    for q in (1, 0):
        yl, zl = (y + q) % 2, (z + q) % 2
        for d in ORDER:
            zt, yt = (z + d) % NZ, (y + d) % NY
            k = d * 2 + q
            in_a[q].append(rcopy(
                slab.at[zt // 2, zt % 2, :, yl, :, pl.ds(0, HALF)], r1a.at[z, yl],
                s1a_s.at[k], s1a_r.at[k], dev(zt, y, c, x),
            ))
            in_b[q].append(rcopy(
                slab.at[:, zl, yt // 2, yt % 2, :, pl.ds(HALF, HALF)], r1b.at[y, zl],
                s1b_s.at[k], s1b_r.at[k], dev(z, yt, c, x),
            ))

    for cp in in_m:
        cp.wait_recv()
    arrive = []
    for d in ORDER + (0,):
        for dc in range(2):
            if d == 0 and dc == 0:
                continue
            to = dev(z, (y + d) % NY, (c + dc) % 2, x)
            arrive.append(rcopy(m1, m2.at[c, y], s2m_s.at[d * 2 + dc], s2m_r.at[d * 2 + dc], to))
    m2[c, y] = m1[...]

    for q, order in ((1, (3, 5, 1, 7)), (0, (4, 2, 6, 0))):
        own[q][0].wait()
        for cp in in_a[q]:
            cp.wait_recv()
        for d in order:
            for dc in range(2):
                if d == 0 and dc == 0:
                    continue
                yt, ct, k = (y + d) % NY, (c + dc) % 2, d * 2 + dc
                arrive.append(rcopy(
                    r1a.at[:, yt % 2, yt // 2, pl.ds(ct * 4, 4), :], r2a.at[y, :, pl.ds(c * 4, 4), :],
                    s2a_s.at[k], s2a_r.at[k], dev(z, yt, ct, x),
                ))
        own[q][1].wait()
        for cp in in_b[q]:
            cp.wait_recv()
        for d in order:
            for dc in range(2):
                if d == 0 and dc == 0:
                    continue
                zt, ct, k = (z + d) % NZ, (c + dc) % 2, d * 2 + dc
                arrive.append(rcopy(
                    r1b.at[:, zt % 2, zt // 2, pl.ds(ct * 4, 4), :], r2b.at[:, z, pl.ds(c * 4, 4), :],
                    s2b_s.at[k], s2b_r.at[k], dev(zt, y, ct, x),
                ))
    l2a = lcopy(r1a.at[:, y % 2, y // 2, pl.ds(c * 4, 4), :], r2a.at[y, :, pl.ds(c * 4, 4), :], loc_sem.at[3])
    l2b = lcopy(r1b.at[:, z % 2, z // 2, pl.ds(c * 4, 4), :], r2b.at[:, z, pl.ds(c * 4, 4), :], loc_sem.at[4])

    n_m = 15
    for cp in arrive[:n_m]:
        cp.wait_recv()
    mt[...] = jnp.transpose(m2[...].reshape(128, 128))
    b4 = mt[pl.ds(y * 8 + c * 4, 4), :]
    w4 = mt[pl.ds(64 + y * 8 + c * 4, 4), :]
    row = lax.broadcasted_iota(jnp.int32, (BPO, 128), 0)
    onehot = jnp.concatenate(
        [jnp.where(row == b4[s:s + 1, :], w4[s:s + 1, :], 0).astype(F32) for s in range(4)], axis=1
    ).astype(BF16)

    for cp in arrive[n_m:]:
        cp.wait_recv()
    l2a.wait()
    l2b.wait()
    fa = r2a.reshape(512, 128)
    fb = r2b.reshape(512, 128)
    rows = jnp.concatenate(
        [
            jnp.concatenate([f[pl.ds(k * 4 + s, 64, stride=8), :] for s in range(4) for k in range(2)], axis=0)
            for f in (fa, fb)
        ],
        axis=1,
    )
    hi = rows.astype(BF16)
    rest = rows - hi.astype(F32)
    mid = rest.astype(BF16)
    low = (rest - mid.astype(F32)).astype(BF16)
    sketch = jnp.dot(onehot, low, preferred_element_type=F32)
    sketch = sketch + jnp.dot(onehot, mid, preferred_element_type=F32)
    sketch = sketch + jnp.dot(onehot, hi, preferred_element_type=F32)
    sk[...] = sketch
    save = lcopy(sk, sk_out, loc_sem.at[8])

    turned = jnp.transpose(sketch)

    def pieces(v):
        first = v.astype(BF16)
        v = v - first.astype(F32)
        second = v.astype(BF16)
        return first, second, (v - second.astype(F32)).astype(BF16)

    ta, tb, tc = pieces(turned)
    sa, sb, sc = pieces(sketch)
    gram = jnp.zeros((BPO, BPO), F32)
    for left, right in ((tc, sa), (ta, sc), (tb, sb), (tb, sa), (ta, sb), (ta, sa)):
        gram = gram + jnp.dot(left, right, preferred_element_type=F32)
    gp[pl.ds(0, 128), :] = gram[:HALF, :HALF]
    gp[pl.ds(128, 128), :] = gram[:HALF, HALF:]
    gp[pl.ds(256, 128), :] = gram[HALF:, HALF:]

    e = x * 2 + c
    near = [(d, dc) for d in (2, 1, 3, 0) for dc in range(2) if d or dc]
    got = []
    for d, dc in near:
        xt, ct = (x + d) % NX, (c + dc) % 2
        at = pl.ds((xt * 2 + ct) * 48, 48)
        got.append(rcopy(gp.at[at], gx.at[d * 2 + dc], x_s.at[d * 2 + dc], x_r.at[d * 2 + dc], dev(z, y, ct, xt)))
    total = gp[pl.ds(pl.multiple_of(e * 48, 8), 48), :]
    for (d, dc), cp in reversed(list(zip(near, got))):
        cp.wait_recv()
        total = total + gx[d * 2 + dc]
    acc[...] = total

    got = []
    for d in ORDER:
        zt = (z + d) % NZ
        got.append(rcopy(acc.at[pl.ds(zt * 6, 6)], gz.at[d, pl.ds(0, 6)], z_s.at[d], z_r.at[d], dev(zt, y, c, x)))
    total = acc[pl.ds(z * 6, 6), :]
    for d, cp in reversed(list(zip(ORDER, got))):
        cp.wait_recv()
        total = total + gz[d, 0:6]
    part[0:6, :] = total

    got = []
    for d in ORDER:
        yt = (y + d) % NY
        got.append(rcopy(part.at[pl.ds(0, 6)], gy.at[y, pl.ds(0, 6)], y_s.at[d], y_r.at[d], dev(z, yt, c, x)))
    gy[y, 0:6] = total
    for cp in got:
        cp.wait_recv()
    quad = [gy[2 * i, 0:6] + gy[2 * i + 1, 0:6] for i in range(4)]
    fin[pl.ds(z * 6, 6), :] = (quad[0] + quad[1]) + (quad[2] + quad[3])

    got = []
    mine = fin.at[pl.ds(z * 6, 6)]
    for d in ORDER:
        zt = (z + d) % NZ
        got.append(rcopy(mine, mine, zg_s.at[d], zg_r.at[d], dev(zt, y, c, x)))
    for cp in got:
        cp.wait_recv()

    got = []
    for d, dc in near:
        xt, ct = (x + d) % NX, (c + dc) % 2
        got.append(
            rcopy(fin, gfull.at[pl.ds(e * 48, 48)], xg_s.at[d * 2 + dc], xg_r.at[d * 2 + dc], dev(z, y, ct, xt))
        )
    gfull[pl.ds(pl.multiple_of(e * 48, 8), 48), :] = fin[...]
    for cp in got:
        cp.wait_recv()
    g_out[...] = gfull[...]
    save.wait()
    for cp in sends:
        cp.wait_send()


def splat(v):
    return jnp.broadcast_to(v, (8, HALF))


def recip(v):
    guess = pl.reciprocal(v, approx=True)
    return guess * (2.0 - v * guess)


def factor_block(mats, spread, k0, emit):
    n = 16
    for p in range(n):
        base = p * 8
        lead = mats[0][base:base + 8, :]
        at = (p % 2) * 64
        for j in range(8):
            spread[at + j * 8:at + j * 8 + 8, :] = splat(lead[:, base + j:base + j + 1])
        d = [[spread[pl.ds(at + j * 8 + i, 8, stride=0), :] for j in range(i + 1)] for i in range(8)]
        rows = [[m[pl.ds(base + i, 8, stride=0), :] for m in mats] for i in range(8)]
        near = list(range(p + 1, min(p + 3, n)))
        blocks = {g: [m[g * 8:g * 8 + 8, :] for m in mats] for g in near}
        side = {g: [splat(blocks[g][0][:, base + j:base + j + 1]) for j in range(8)] for g in near}
        final = []
        for b in range(0, 8, 2):
            p00, p10, p11 = d[b][b], d[b + 1][b], d[b + 1][b + 1]
            inv = recip(p00 * p11 - p10 * p10)
            x0, x1 = rows[b], rows[b + 1]
            for g in near:
                v = side[g]
                n0 = p11 * v[b] - p10 * v[b + 1]
                n1 = p00 * v[b + 1] - p10 * v[b]
                blocks[g] = [t - (n0 * x0[k] + n1 * x1[k]) * inv for k, t in enumerate(blocks[g])]
                if b < 6:
                    n0, n1 = n0 * inv, n1 * inv
                for i in range(b + 2, 8):
                    v[i] = v[i] - (n0 * d[i][b] + n1 * d[i][b + 1])
            for i in range(b + 2, 8):
                n0 = p11 * d[i][b] - p10 * d[i][b + 1]
                n1 = p00 * d[i][b + 1] - p10 * d[i][b]
                for j in range(b + 2, i + 1):
                    d[i][j] = d[i][j] - (n0 * d[j][b] + n1 * d[j][b + 1]) * inv
                n0, n1 = n0 * inv, n1 * inv
                rows[i] = [t - (n0 * x0[k] + n1 * x1[k]) for k, t in enumerate(rows[i])]
            r0 = lax.rsqrt(p00)
            low = p10 * r0
            r1 = lax.rsqrt(p11 - low * low)
            first = [t * r0 for t in x0]
            final.append(first)
            final.append([(t - low * first[k]) * r1 for k, t in enumerate(x1)])
        for g in near:
            for k, m in enumerate(mats):
                m[g * 8:g * 8 + 8, :] = blocks[g][k]
        for j in range(8):
            emit(k0 + base + j, base + j, [t[0:1, :] for t in final[j]])
        if p + 3 < n:
            first = (p + 3) * 8
            panel = [
                jnp.concatenate([final[j][k][0:1, :] for j in range(8)], axis=0) for k in range(len(mats))
            ]
            for k, m in enumerate(mats):
                less = lax.dot_general(
                    panel[0], panel[k], (((0,), (0,)), ((), ())),
                    precision=lax.Precision.HIGHEST, preferred_element_type=F32,
                )
                m[first:, :] = m[first:, :] - less[first:, :]


def factor_kernel(scale, g_ref, sk_ref, f_out, sk_out, a0, a1, spread, sem):
    cp = pltpu.make_async_copy(sk_ref, sk_out, sem)
    cp.start()
    lane = lax.broadcasted_iota(jnp.int32, (8, HALF), 1)
    sub = lax.broadcasted_iota(jnp.int32, (8, HALF), 0)
    across, down = [], []
    for at in (0, 256):
        picked = [jnp.where(lane == sub + p * 8, g_ref[at + p * 8:at + p * 8 + 8, :], 0.0) for p in range(16)]
        down.append([lax.rsqrt(splat(jnp.sum(t, axis=1, keepdims=True))) for t in picked])
        while len(picked) > 1:
            picked = [picked[i] + picked[i + 1] for i in range(0, len(picked), 2)]
        across.append(splat(jnp.sum(picked[0], axis=0, keepdims=True)))
    scaled = [lax.rsqrt(v) for v in across]
    back = [jnp.sqrt(v * scale) for v in across]

    def emit(first):
        def put(at, diagonal, values):
            for k, v in enumerate(values):
                v = v * back[first + k][0:1, :]
                if k == 0:
                    v = jnp.where(lane[0:1, :] >= diagonal, v, 0.0)
                f_out[at:at + 1, (first + k) * HALF:(first + k + 1) * HALF] = v
        return put

    for p in range(16):
        at = p * 8
        a0[at:at + 8, :] = g_ref[at:at + 8, :] * (down[0][p] * scaled[0])
        a1[at:at + 8, :] = g_ref[128 + at:128 + at + 8, :] * (down[0][p] * scaled[1])
    f_out[128:256, 0:128] = jnp.zeros((128, 128), F32)
    factor_block([a0, a1], spread, 0, emit(0))
    corner = f_out[0:128, 128:256]
    less = lax.dot_general(
        corner, corner, (((0,), (0,)), ((), ())), precision=lax.Precision.HIGHEST, preferred_element_type=F32
    )
    for p in range(16):
        at = p * 8
        left = g_ref[256 + at:256 + at + 8, :] - less[at:at + 8, :] * (1.0 / scale)
        a0[at:at + 8, :] = left * (down[1][p] * scaled[1])
    factor_block([a0], spread, 128, emit(1))
    cp.wait()


def body(slab, buckets, signs, counts):
    owners = lax.axis_size("rows")
    capacity = slab.shape[1] // owners
    width = slab.shape[2]
    vm = pl.BlockSpec(memory_space=pltpu.VMEM)
    hbm = pl.BlockSpec(memory_space=pltpu.HBM)
    dma = pltpu.SemaphoreType.DMA
    sketch, gram = pl.pallas_call(
        gram_kernel,
        out_shape=(jax.ShapeDtypeStruct((BPO, width), F32), jax.ShapeDtypeStruct((384, 128), F32)),
        in_specs=[hbm] * 4,
        out_specs=(hbm, vm),
        scratch_shapes=[
            pltpu.VMEM((4, 2, 4, 2, 8, 256), F32),
            pltpu.VMEM((1, 512), jnp.int32),
            pltpu.VMEM((1, 512), jnp.int32),
            pltpu.VMEM((1, 128), jnp.int32),
            pltpu.VMEM((256, 256), F32),
            pltpu.VMEM((8, 128), jnp.int32),
            pltpu.VMEM((8, 2, 4, 8, 128), F32),
            pltpu.VMEM((8, 2, 4, 8, 128), F32),
            pltpu.VMEM((8, 8, 8, 128), F32),
            pltpu.VMEM((8, 8, 8, 128), F32),
            pltpu.VMEM((8, 128), jnp.int32),
            pltpu.VMEM((2, 8, 8, 128), jnp.int32),
            pltpu.VMEM((128, 128), jnp.int32),
            pltpu.VMEM((384, 128), F32),
            pltpu.VMEM((8, 48, 128), F32),
            pltpu.VMEM((48, 128), F32),
            pltpu.VMEM((8, 8, 128), F32),
            pltpu.VMEM((8, 128), F32),
            pltpu.VMEM((8, 8, 128), F32),
            pltpu.VMEM((48, 128), F32),
            pltpu.VMEM((384, 128), F32),
            dma((13,)),
            dma((16,)), dma((16,)), dma((16,)), dma((16,)), dma((8,)), dma((8,)),
            dma((16,)), dma((16,)), dma((16,)), dma((16,)), dma((16,)), dma((16,)),
            dma((8,)), dma((8,)), dma((8,)), dma((8,)), dma((8,)), dma((8,)),
            dma((8,)), dma((8,)), dma((8,)), dma((8,)),
        ],
        compiler_params=pltpu.CompilerParams(
            collective_id=0, has_side_effects=True, vmem_limit_bytes=60 * 1024 * 1024
        ),
    )(slab.reshape(4, 2, 4, 2, 8, width), buckets, signs, counts)
    slots = float(lax.axis_size("grp") * owners * owners * capacity)
    factor, sketch = pl.pallas_call(
        lambda *refs: factor_kernel(1.0 / slots, *refs),
        out_shape=(jax.ShapeDtypeStruct((width, width), F32), jax.ShapeDtypeStruct((BPO, width), F32)),
        in_specs=[vm, hbm],
        out_specs=(vm, hbm),
        scratch_shapes=[
            pltpu.VMEM((HALF, HALF), F32),
            pltpu.VMEM((HALF, HALF), F32),
            pltpu.VMEM((HALF, HALF), F32),
            pltpu.SemaphoreType.DMA,
        ],
        compiler_params=pltpu.CompilerParams(vmem_limit_bytes=60 * 1024 * 1024),
    )(gram, sketch)
    return (sketch.reshape(1, BPO, width), factor)


def solution(mesh):
    in_specs = (P("grp", "rows", None), P("grp", "rows"), P("grp", "rows"), P("grp", "rows"))
    out_specs = (P("grp", "rows", None), P())
    return jax.shard_map(body, mesh=mesh, in_specs=in_specs, out_specs=out_specs, check_vma=False)
```

```python
import jax
import jax.numpy as jnp
from jax import lax
from jax.experimental import pallas as pl
from jax.experimental.pallas import tpu as pltpu
from jax.sharding import PartitionSpec as P

NZ = 8
NY = 8
NX = 4
BPO = 256
HALF = 128
F32 = jnp.float32
BF16 = jnp.bfloat16
MESH = pl.DeviceIdType.MESH
ORDER = (4, 3, 5, 2, 6, 1, 7)


def gram_kernel(
    slab, buckets_hbm, signs_hbm, counts_hbm, sk_out, g_out,
    buckets, signs, counts, sk, meta, r1a, r1b, r2a, r2b, m1, m2, mt, gp, gx, acc, gz, part, gy, fin, gfull,
    loc_sem, s1a_s, s1a_r, s1b_s, s1b_r, s1m_s, s1m_r, s2a_s, s2a_r, s2b_s, s2b_r, s2m_s, s2m_r,
    x_s, x_r, z_s, z_r, y_s, y_r, zg_s, zg_r, xg_s, xg_r,
):
    r = lax.axis_index("rows")
    x = lax.axis_index("grp")
    z = r // 16
    y = (r // 2) % 8
    c = r % 2

    def dev(zz, yy, cc, xx):
        return ((zz * NY + yy) * 2 + cc, xx)

    barrier = pltpu.get_barrier_semaphore()
    peers = [dev(z, y, 1 - c, x)]
    for d in range(1, 8):
        for dc in range(2):
            peers.append(dev((z + d) % NZ, y, (c + dc) % 2, x))
            peers.append(dev(z, (y + d) % NY, (c + dc) % 2, x))
    for d in range(1, 4):
        for dc in range(2):
            peers.append(dev(z, y, (c + dc) % 2, (x + d) % NX))

    def lcopy(src, dst, sem):
        cp = pltpu.make_async_copy(src, dst, sem)
        cp.start()
        return cp

    small = [
        lcopy(counts_hbm, counts, loc_sem.at[5]),
        lcopy(signs_hbm, signs, loc_sem.at[6]),
        lcopy(buckets_hbm, buckets, loc_sem.at[7]),
    ]
    for p in peers:
        pl.semaphore_signal(barrier, inc=1, device_id=p, device_id_type=MESH)

    sends = []

    def rcopy(src, dst, ss, rs, to):
        cp = pltpu.make_async_remote_copy(
            src_ref=src, dst_ref=dst, send_sem=ss, recv_sem=rs, device_id=to, device_id_type=MESH
        )
        cp.start()
        sends.append(cp)
        return cp

    own = {}
    for q in range(2):
        yl, zl = (y + q) % 2, (z + q) % 2
        own[q] = (
            lcopy(slab.at[z // 2, z % 2, :, yl, :, pl.ds(0, HALF)], r1a.at[z, yl], loc_sem.at[9 + q]),
            lcopy(slab.at[:, zl, y // 2, y % 2, :, pl.ds(HALF, HALF)], r1b.at[y, zl], loc_sem.at[11 + q]),
        )
    pl.semaphore_wait(barrier, len(peers))

    in_a, in_b = {0: [], 1: []}, {0: [], 1: []}

    def first_stage(q):
        yl, zl = (y + q) % 2, (z + q) % 2
        for d in ORDER:
            zt, yt = (z + d) % NZ, (y + d) % NY
            k = d * 2 + q
            in_a[q].append(rcopy(
                slab.at[zt // 2, zt % 2, :, yl, :, pl.ds(0, HALF)], r1a.at[z, yl],
                s1a_s.at[k], s1a_r.at[k], dev(zt, y, c, x),
            ))
            in_b[q].append(rcopy(
                slab.at[:, zl, yt // 2, yt % 2, :, pl.ds(HALF, HALF)], r1b.at[y, zl],
                s1b_s.at[k], s1b_r.at[k], dev(z, yt, c, x),
            ))

    first_stage(1)
    slot = lax.broadcasted_iota(jnp.int32, (HALF, 512), 1)
    pair = lax.broadcasted_iota(jnp.int32, (HALF, 512), 0)
    spread = jnp.where(slot // 4 == pair, 1.0, 0.0).astype(BF16)
    for cp in small:
        cp.wait()
    limit = jnp.dot(
        jnp.broadcast_to(counts[...], (8, HALF)).astype(F32).astype(BF16), spread, preferred_element_type=F32
    )[0:1, :]
    place = lax.broadcasted_iota(jnp.int32, (1, 512), 1) % 4
    weight = jnp.where(place.astype(F32) < limit, signs[...], 0)
    for t in range(NZ):
        meta[t:t + 1, 0:64] = buckets[0:1, t * 64:t * 64 + 64]
        meta[t:t + 1, 64:128] = weight[0:1, t * 64:t * 64 + 64]
    m1[pl.ds(z, 1), :] = meta[pl.ds(z, 1), :]
    in_m = []
    for d in ORDER:
        zt = (z + d) % NZ
        in_m.append(rcopy(meta.at[pl.ds(zt, 1)], m1.at[pl.ds(z, 1)], s1m_s.at[d], s1m_r.at[d], dev(zt, y, c, x)))
    first_stage(0)
    arrive, arrive_m = [], []

    def second_stage(q, order):
        own[q][0].wait()
        for cp in in_a[q]:
            cp.wait_recv()
        for d in order:
            for dc in range(2):
                if d == 0 and dc == 0:
                    continue
                yt, ct, k = (y + d) % NY, (c + dc) % 2, d * 2 + dc
                arrive.append(rcopy(
                    r1a.at[:, yt % 2, yt // 2, pl.ds(ct * 4, 4), :], r2a.at[y, :, pl.ds(c * 4, 4), :],
                    s2a_s.at[k], s2a_r.at[k], dev(z, yt, ct, x),
                ))
        own[q][1].wait()
        for cp in in_b[q]:
            cp.wait_recv()
        for d in order:
            for dc in range(2):
                if d == 0 and dc == 0:
                    continue
                zt, ct, k = (z + d) % NZ, (c + dc) % 2, d * 2 + dc
                arrive.append(rcopy(
                    r1b.at[:, zt % 2, zt // 2, pl.ds(ct * 4, 4), :], r2b.at[:, z, pl.ds(c * 4, 4), :],
                    s2b_s.at[k], s2b_r.at[k], dev(zt, y, ct, x),
                ))
    second_stage(1, (3, 5, 1, 7))
    for cp in in_m:
        cp.wait_recv()
    for d in ORDER + (0,):
        for dc in range(2):
            if d == 0 and dc == 0:
                continue
            to = dev(z, (y + d) % NY, (c + dc) % 2, x)
            arrive_m.append(rcopy(m1, m2.at[c, y], s2m_s.at[d * 2 + dc], s2m_r.at[d * 2 + dc], to))
    m2[c, y] = m1[...]
    second_stage(0, (4, 2, 6, 0))
    l2a = lcopy(r1a.at[:, y % 2, y // 2, pl.ds(c * 4, 4), :], r2a.at[y, :, pl.ds(c * 4, 4), :], loc_sem.at[3])
    l2b = lcopy(r1b.at[:, z % 2, z // 2, pl.ds(c * 4, 4), :], r2b.at[:, z, pl.ds(c * 4, 4), :], loc_sem.at[4])

    for cp in arrive_m:
        cp.wait_recv()
    mt[...] = jnp.transpose(m2[...].reshape(128, 128))
    b4 = mt[pl.ds(y * 8 + c * 4, 4), :]
    w4 = mt[pl.ds(64 + y * 8 + c * 4, 4), :]
    row = lax.broadcasted_iota(jnp.int32, (BPO, 128), 0)
    onehot = jnp.concatenate(
        [jnp.where(row == b4[s:s + 1, :], w4[s:s + 1, :], 0).astype(F32) for s in range(4)], axis=1
    ).astype(BF16)

    for cp in arrive:
        cp.wait_recv()
    l2a.wait()
    l2b.wait()
    fa = r2a.reshape(512, 128)
    fb = r2b.reshape(512, 128)
    rows = jnp.concatenate(
        [
            jnp.concatenate([f[pl.ds(k * 4 + s, 64, stride=8), :] for s in range(4) for k in range(2)], axis=0)
            for f in (fa, fb)
        ],
        axis=1,
    )
    hi = rows.astype(BF16)
    rest = rows - hi.astype(F32)
    mid = rest.astype(BF16)
    low = (rest - mid.astype(F32)).astype(BF16)
    sketch = jnp.dot(onehot, low, preferred_element_type=F32)
    sketch = sketch + jnp.dot(onehot, mid, preferred_element_type=F32)
    sketch = sketch + jnp.dot(onehot, hi, preferred_element_type=F32)
    sk[...] = sketch
    save = lcopy(sk, sk_out, loc_sem.at[8])

    turned = jnp.transpose(sketch)

    def pieces(v):
        first = v.astype(BF16)
        v = v - first.astype(F32)
        second = v.astype(BF16)
        return first, second, (v - second.astype(F32)).astype(BF16)

    ta, tb, tc = pieces(turned)
    sa, sb, sc = pieces(sketch)
    gram = jnp.zeros((BPO, BPO), F32)
    for left, right in ((tc, sa), (ta, sc), (tb, sb), (tb, sa), (ta, sb), (ta, sa)):
        gram = gram + jnp.dot(left, right, preferred_element_type=F32)
    gp[pl.ds(0, 128), :] = gram[:HALF, :HALF]
    gp[pl.ds(128, 128), :] = gram[:HALF, HALF:]
    gp[pl.ds(256, 128), :] = gram[HALF:, HALF:]

    e = x * 2 + c
    near = [(d, dc) for d in (2, 1, 3, 0) for dc in range(2) if d or dc]
    got = []
    for d, dc in near:
        xt, ct = (x + d) % NX, (c + dc) % 2
        at = pl.ds((xt * 2 + ct) * 48, 48)
        got.append(rcopy(gp.at[at], gx.at[d * 2 + dc], x_s.at[d * 2 + dc], x_r.at[d * 2 + dc], dev(z, y, ct, xt)))
    total = gp[pl.ds(pl.multiple_of(e * 48, 8), 48), :]
    for (d, dc), cp in reversed(list(zip(near, got))):
        cp.wait_recv()
        total = total + gx[d * 2 + dc]
    acc[...] = total

    got = []
    for d in ORDER:
        zt = (z + d) % NZ
        got.append(rcopy(acc.at[pl.ds(zt * 6, 6)], gz.at[d, pl.ds(0, 6)], z_s.at[d], z_r.at[d], dev(zt, y, c, x)))
    total = acc[pl.ds(z * 6, 6), :]
    for d, cp in reversed(list(zip(ORDER, got))):
        cp.wait_recv()
        total = total + gz[d, 0:6]
    part[0:6, :] = total

    got = []
    for d in ORDER:
        yt = (y + d) % NY
        got.append(rcopy(part.at[pl.ds(0, 6)], gy.at[y, pl.ds(0, 6)], y_s.at[d], y_r.at[d], dev(z, yt, c, x)))
    gy[y, 0:6] = total
    for cp in got:
        cp.wait_recv()
    quad = [gy[2 * i, 0:6] + gy[2 * i + 1, 0:6] for i in range(4)]
    fin[pl.ds(z * 6, 6), :] = (quad[0] + quad[1]) + (quad[2] + quad[3])

    got = []
    mine = fin.at[pl.ds(z * 6, 6)]
    for d in ORDER:
        zt = (z + d) % NZ
        got.append(rcopy(mine, mine, zg_s.at[d], zg_r.at[d], dev(zt, y, c, x)))
    for cp in got:
        cp.wait_recv()

    got = []
    for d, dc in near:
        xt, ct = (x + d) % NX, (c + dc) % 2
        got.append(
            rcopy(fin, gfull.at[pl.ds(e * 48, 48)], xg_s.at[d * 2 + dc], xg_r.at[d * 2 + dc], dev(z, y, ct, xt))
        )
    gfull[pl.ds(pl.multiple_of(e * 48, 8), 48), :] = fin[...]
    for cp in got:
        cp.wait_recv()
    g_out[...] = gfull[...]
    save.wait()
    for cp in sends:
        cp.wait_send()


def splat(v):
    return jnp.broadcast_to(v, (8, HALF))


def recip(v):
    guess = pl.reciprocal(v, approx=True)
    return guess * (2.0 - v * guess)


def factor_block(mats, spread, turn, k0, emit):
    n = 16
    for p in range(n):
        base = p * 8
        at = (p % 2) * 64
        if p == 0:
            ahead = [splat(mats[0][0:8, :][:, j:j + 1]) for j in range(8)]
        for j in range(8):
            spread[at + j * 8:at + j * 8 + 8, :] = ahead[j]
        d = [[spread[pl.ds(at + j * 8 + i, 8, stride=0), :] for j in range(i + 1)] for i in range(8)]
        rows = [[m[pl.ds(base + i, 8, stride=0), :] for m in mats] for i in range(8)]
        near = list(range(p + 1, min(p + 3, n)))
        blocks = {g: [m[g * 8:g * 8 + 8, :] for m in mats] for g in near}
        side = {g: [splat(blocks[g][0][:, base + j:base + j + 1]) for j in range(8)] for g in near}
        if near:
            ahead = [splat(blocks[p + 1][0][:, base + 8 + j:base + 9 + j]) for j in range(8)]
        final = []
        for b in range(0, 8, 2):
            p00, p10, p11 = d[b][b], d[b + 1][b], d[b + 1][b + 1]
            inv = recip(p00 * p11 - p10 * p10)
            x0, x1 = rows[b], rows[b + 1]
            for g in near:
                v = side[g]
                n0 = p11 * v[b] - p10 * v[b + 1]
                n1 = p00 * v[b + 1] - p10 * v[b]
                blocks[g] = [t - (n0 * x0[k] + n1 * x1[k]) * inv for k, t in enumerate(blocks[g])]
                if g == p + 1:
                    to = at + b * 8
                    turn[to:to + 8, :] = v[b]
                    turn[to + 8:to + 16, :] = v[b + 1]
                    for j in range(8):
                        s0 = turn[pl.ds(to + j, 8, stride=0), :]
                        s1 = turn[pl.ds(to + 8 + j, 8, stride=0), :]
                        ahead[j] = ahead[j] - (n0 * s0 + n1 * s1) * inv
                if b < 6:
                    n0, n1 = n0 * inv, n1 * inv
                for i in range(b + 2, 8):
                    v[i] = v[i] - (n0 * d[i][b] + n1 * d[i][b + 1])
            for i in range(b + 2, 8):
                n0 = p11 * d[i][b] - p10 * d[i][b + 1]
                n1 = p00 * d[i][b + 1] - p10 * d[i][b]
                for j in range(b + 2, i + 1):
                    d[i][j] = d[i][j] - (n0 * d[j][b] + n1 * d[j][b + 1]) * inv
                n0, n1 = n0 * inv, n1 * inv
                rows[i] = [t - (n0 * x0[k] + n1 * x1[k]) for k, t in enumerate(rows[i])]
            r0 = lax.rsqrt(p00)
            low = p10 * r0
            r1 = lax.rsqrt(p11 - low * low)
            first = [t * r0 for t in x0]
            final.append(first)
            final.append([(t - low * first[k]) * r1 for k, t in enumerate(x1)])
        for g in near:
            for k, m in enumerate(mats):
                m[g * 8:g * 8 + 8, :] = blocks[g][k]
        for j in range(8):
            emit(k0 + base + j, base + j, [t[0:1, :] for t in final[j]])
        if p + 3 < n:
            first = (p + 3) * 8
            panel = [
                jnp.concatenate([final[j][k][0:1, :] for j in range(8)], axis=0) for k in range(len(mats))
            ]
            for k, m in enumerate(mats):
                less = lax.dot_general(
                    panel[0], panel[k], (((0,), (0,)), ((), ())),
                    precision=lax.Precision.HIGHEST, preferred_element_type=F32,
                )
                m[first:, :] = m[first:, :] - less[first:, :]


def factor_kernel(scale, g_ref, sk_ref, f_out, sk_out, a0, a1, spread, turn, sem):
    cp = pltpu.make_async_copy(sk_ref, sk_out, sem)
    cp.start()
    lane = lax.broadcasted_iota(jnp.int32, (8, HALF), 1)
    sub = lax.broadcasted_iota(jnp.int32, (8, HALF), 0)
    across, down = [], []
    for at in (0, 256):
        picked = [jnp.where(lane == sub + p * 8, g_ref[at + p * 8:at + p * 8 + 8, :], 0.0) for p in range(16)]
        down.append([lax.rsqrt(splat(jnp.sum(t, axis=1, keepdims=True))) for t in picked])
        while len(picked) > 1:
            picked = [picked[i] + picked[i + 1] for i in range(0, len(picked), 2)]
        across.append(splat(jnp.sum(picked[0], axis=0, keepdims=True)))
    scaled = [lax.rsqrt(v) for v in across]
    back = [jnp.sqrt(v * scale) for v in across]

    def emit(first):
        def put(at, diagonal, values):
            for k, v in enumerate(values):
                v = v * back[first + k][0:1, :]
                if k == 0:
                    v = jnp.where(lane[0:1, :] >= diagonal, v, 0.0)
                f_out[at:at + 1, (first + k) * HALF:(first + k + 1) * HALF] = v
        return put

    for p in range(16):
        at = p * 8
        a0[at:at + 8, :] = g_ref[at:at + 8, :] * (down[0][p] * scaled[0])
        a1[at:at + 8, :] = g_ref[128 + at:128 + at + 8, :] * (down[0][p] * scaled[1])
    f_out[128:256, 0:128] = jnp.zeros((128, 128), F32)
    factor_block([a0, a1], spread, turn, 0, emit(0))
    corner = f_out[0:128, 128:256]
    less = lax.dot_general(
        corner, corner, (((0,), (0,)), ((), ())), precision=lax.Precision.HIGHEST, preferred_element_type=F32
    )
    for p in range(16):
        at = p * 8
        left = g_ref[256 + at:256 + at + 8, :] - less[at:at + 8, :] * (1.0 / scale)
        a0[at:at + 8, :] = left * (down[1][p] * scaled[1])
    factor_block([a0], spread, turn, 128, emit(1))
    cp.wait()


def body(slab, buckets, signs, counts):
    owners = lax.axis_size("rows")
    capacity = slab.shape[1] // owners
    width = slab.shape[2]
    vm = pl.BlockSpec(memory_space=pltpu.VMEM)
    hbm = pl.BlockSpec(memory_space=pltpu.HBM)
    dma = pltpu.SemaphoreType.DMA
    sketch, gram = pl.pallas_call(
        gram_kernel,
        out_shape=(jax.ShapeDtypeStruct((BPO, width), F32), jax.ShapeDtypeStruct((384, 128), F32)),
        in_specs=[hbm] * 4,
        out_specs=(hbm, vm),
        scratch_shapes=[
            pltpu.VMEM((1, 512), jnp.int32),
            pltpu.VMEM((1, 512), jnp.int32),
            pltpu.VMEM((1, 128), jnp.int32),
            pltpu.VMEM((256, 256), F32),
            pltpu.VMEM((8, 128), jnp.int32),
            pltpu.VMEM((8, 2, 4, 8, 128), F32),
            pltpu.VMEM((8, 2, 4, 8, 128), F32),
            pltpu.VMEM((8, 8, 8, 128), F32),
            pltpu.VMEM((8, 8, 8, 128), F32),
            pltpu.VMEM((8, 128), jnp.int32),
            pltpu.VMEM((2, 8, 8, 128), jnp.int32),
            pltpu.VMEM((128, 128), jnp.int32),
            pltpu.VMEM((384, 128), F32),
            pltpu.VMEM((8, 48, 128), F32),
            pltpu.VMEM((48, 128), F32),
            pltpu.VMEM((8, 8, 128), F32),
            pltpu.VMEM((8, 128), F32),
            pltpu.VMEM((8, 8, 128), F32),
            pltpu.VMEM((48, 128), F32),
            pltpu.VMEM((384, 128), F32),
            dma((13,)),
            dma((16,)), dma((16,)), dma((16,)), dma((16,)), dma((8,)), dma((8,)),
            dma((16,)), dma((16,)), dma((16,)), dma((16,)), dma((16,)), dma((16,)),
            dma((8,)), dma((8,)), dma((8,)), dma((8,)), dma((8,)), dma((8,)),
            dma((8,)), dma((8,)), dma((8,)), dma((8,)),
        ],
        compiler_params=pltpu.CompilerParams(
            collective_id=0, has_side_effects=True, vmem_limit_bytes=60 * 1024 * 1024
        ),
    )(slab.reshape(4, 2, 4, 2, 8, width), buckets, signs, counts)
    slots = float(lax.axis_size("grp") * owners * owners * capacity)
    factor, sketch = pl.pallas_call(
        lambda *refs: factor_kernel(1.0 / slots, *refs),
        out_shape=(jax.ShapeDtypeStruct((width, width), F32), jax.ShapeDtypeStruct((BPO, width), F32)),
        in_specs=[vm, hbm],
        out_specs=(vm, hbm),
        scratch_shapes=[
            pltpu.VMEM((HALF, HALF), F32),
            pltpu.VMEM((HALF, HALF), F32),
            pltpu.VMEM((HALF, HALF), F32),
            pltpu.VMEM((HALF, HALF), F32),
            pltpu.SemaphoreType.DMA,
        ],
        compiler_params=pltpu.CompilerParams(vmem_limit_bytes=60 * 1024 * 1024),
    )(gram, sketch)
    return (sketch.reshape(1, BPO, width), factor)


def solution(mesh):
    in_specs = (P("grp", "rows", None), P("grp", "rows"), P("grp", "rows"), P("grp", "rows"))
    out_specs = (P("grp", "rows", None), P())
    return jax.shard_map(body, mesh=mesh, in_specs=in_specs, out_specs=out_specs, check_vma=False)
```

```python
import jax
import jax.numpy as jnp
from jax import lax
from jax.experimental import pallas as pl
from jax.experimental.pallas import tpu as pltpu
from jax.sharding import PartitionSpec as P

NZ = 8
NY = 8
NX = 4
BPO = 256
HALF = 128
F32 = jnp.float32
BF16 = jnp.bfloat16
MESH = pl.DeviceIdType.MESH
ORDER = (4, 3, 5, 2, 6, 1, 7)


def gram_kernel(
    slab_hbm, buckets_hbm, signs_hbm, counts_hbm, sk_out, g_out,
    slab, buckets, signs, counts, sk, meta, r1a, r1b, r2a, r2b, m1, m2, mt, gp, gx, acc, gz, part, gy, fin, gfull,
    loc_sem, s1a_s, s1a_r, s1b_s, s1b_r, s1m_s, s1m_r, s2a_s, s2a_r, s2b_s, s2b_r, s2m_s, s2m_r,
    x_s, x_r, z_s, z_r, y_s, y_r, zg_s, zg_r, xg_s, xg_r,
):
    r = lax.axis_index("rows")
    x = lax.axis_index("grp")
    z = r // 16
    y = (r // 2) % 8
    c = r % 2

    def dev(zz, yy, cc, xx):
        return ((zz * NY + yy) * 2 + cc, xx)

    barrier = pltpu.get_barrier_semaphore()
    peers = [dev(z, y, 1 - c, x)]
    for d in range(1, 8):
        for dc in range(2):
            peers.append(dev((z + d) % NZ, y, (c + dc) % 2, x))
            peers.append(dev(z, (y + d) % NY, (c + dc) % 2, x))
    for d in range(1, 4):
        for dc in range(2):
            peers.append(dev(z, y, (c + dc) % 2, (x + d) % NX))
    for p in peers:
        pl.semaphore_signal(barrier, inc=1, device_id=p, device_id_type=MESH)

    sends = []

    def rcopy(src, dst, ss, rs, to):
        cp = pltpu.make_async_remote_copy(
            src_ref=src, dst_ref=dst, send_sem=ss, recv_sem=rs, device_id=to, device_id_type=MESH
        )
        cp.start()
        sends.append(cp)
        return cp

    def lcopy(src, dst, sem):
        cp = pltpu.make_async_copy(src, dst, sem)
        cp.start()
        return cp

    load = lcopy(slab_hbm, slab, loc_sem.at[2])
    small = [
        lcopy(counts_hbm, counts, loc_sem.at[5]),
        lcopy(signs_hbm, signs, loc_sem.at[6]),
        lcopy(buckets_hbm, buckets, loc_sem.at[7]),
    ]
    slot = lax.broadcasted_iota(jnp.int32, (HALF, 512), 1)
    pair = lax.broadcasted_iota(jnp.int32, (HALF, 512), 0)
    spread = jnp.where(slot // 4 == pair, 1.0, 0.0).astype(BF16)
    for cp in small:
        cp.wait()
    limit = jnp.dot(
        jnp.broadcast_to(counts[...], (8, HALF)).astype(F32).astype(BF16), spread, preferred_element_type=F32
    )[0:1, :]
    place = lax.broadcasted_iota(jnp.int32, (1, 512), 1) % 4
    weight = jnp.where(place.astype(F32) < limit, signs[...], 0)
    for t in range(NZ):
        meta[t:t + 1, 0:64] = buckets[0:1, t * 64:t * 64 + 64]
        meta[t:t + 1, 64:128] = weight[0:1, t * 64:t * 64 + 64]
    load.wait()
    own = {}
    for q in range(2):
        yl, zl = (y + q) % 2, (z + q) % 2
        own[q] = (
            lcopy(slab.at[z // 2, z % 2, :, yl, :, pl.ds(0, HALF)], r1a.at[z, yl], loc_sem.at[9 + q]),
            lcopy(slab.at[:, zl, y // 2, y % 2, :, pl.ds(HALF, HALF)], r1b.at[y, zl], loc_sem.at[11 + q]),
        )
    m1[pl.ds(z, 1), :] = meta[pl.ds(z, 1), :]
    pl.semaphore_wait(barrier, len(peers))

    in_m = []
    for d in ORDER:
        zt = (z + d) % NZ
        in_m.append(rcopy(meta.at[pl.ds(zt, 1)], m1.at[pl.ds(z, 1)], s1m_s.at[d], s1m_r.at[d], dev(zt, y, c, x)))
    in_a, in_b = {0: [], 1: []}, {0: [], 1: []}
    for q in (1, 0):
        yl, zl = (y + q) % 2, (z + q) % 2
        for d in ORDER:
            zt, yt = (z + d) % NZ, (y + d) % NY
            k = d * 2 + q
            in_a[q].append(rcopy(
                slab.at[zt // 2, zt % 2, :, yl, :, pl.ds(0, HALF)], r1a.at[z, yl],
                s1a_s.at[k], s1a_r.at[k], dev(zt, y, c, x),
            ))
            in_b[q].append(rcopy(
                slab.at[:, zl, yt // 2, yt % 2, :, pl.ds(HALF, HALF)], r1b.at[y, zl],
                s1b_s.at[k], s1b_r.at[k], dev(z, yt, c, x),
            ))

    for cp in in_m:
        cp.wait_recv()
    arrive = []
    for d in ORDER + (0,):
        for dc in range(2):
            if d == 0 and dc == 0:
                continue
            to = dev(z, (y + d) % NY, (c + dc) % 2, x)
            arrive.append(rcopy(m1, m2.at[c, y], s2m_s.at[d * 2 + dc], s2m_r.at[d * 2 + dc], to))
    m2[c, y] = m1[...]

    for q, order in ((1, (3, 5, 1, 7)), (0, (4, 2, 6, 0))):
        own[q][0].wait()
        for cp in in_a[q]:
            cp.wait_recv()
        for d in order:
            for dc in range(2):
                if d == 0 and dc == 0:
                    continue
                yt, ct, k = (y + d) % NY, (c + dc) % 2, d * 2 + dc
                arrive.append(rcopy(
                    r1a.at[:, yt % 2, yt // 2, pl.ds(ct * 4, 4), :], r2a.at[y, :, pl.ds(c * 4, 4), :],
                    s2a_s.at[k], s2a_r.at[k], dev(z, yt, ct, x),
                ))
        own[q][1].wait()
        for cp in in_b[q]:
            cp.wait_recv()
        for d in order:
            for dc in range(2):
                if d == 0 and dc == 0:
                    continue
                zt, ct, k = (z + d) % NZ, (c + dc) % 2, d * 2 + dc
                arrive.append(rcopy(
                    r1b.at[:, zt % 2, zt // 2, pl.ds(ct * 4, 4), :], r2b.at[:, z, pl.ds(c * 4, 4), :],
                    s2b_s.at[k], s2b_r.at[k], dev(zt, y, ct, x),
                ))
    l2a = lcopy(r1a.at[:, y % 2, y // 2, pl.ds(c * 4, 4), :], r2a.at[y, :, pl.ds(c * 4, 4), :], loc_sem.at[3])
    l2b = lcopy(r1b.at[:, z % 2, z // 2, pl.ds(c * 4, 4), :], r2b.at[:, z, pl.ds(c * 4, 4), :], loc_sem.at[4])

    n_m = 15
    for cp in arrive[:n_m]:
        cp.wait_recv()
    mt[...] = jnp.transpose(m2[...].reshape(128, 128))
    b4 = mt[pl.ds(y * 8 + c * 4, 4), :]
    w4 = mt[pl.ds(64 + y * 8 + c * 4, 4), :]
    row = lax.broadcasted_iota(jnp.int32, (BPO, 128), 0)
    onehot = jnp.concatenate(
        [jnp.where(row == b4[s:s + 1, :], w4[s:s + 1, :], 0).astype(F32) for s in range(4)], axis=1
    ).astype(BF16)

    for cp in arrive[n_m:]:
        cp.wait_recv()
    l2a.wait()
    l2b.wait()
    fa = r2a.reshape(512, 128)
    fb = r2b.reshape(512, 128)
    rows = jnp.concatenate(
        [
            jnp.concatenate([f[pl.ds(k * 4 + s, 64, stride=8), :] for s in range(4) for k in range(2)], axis=0)
            for f in (fa, fb)
        ],
        axis=1,
    )
    hi = rows.astype(BF16)
    rest = rows - hi.astype(F32)
    mid = rest.astype(BF16)
    low = (rest - mid.astype(F32)).astype(BF16)
    sketch = jnp.dot(onehot, low, preferred_element_type=F32)
    sketch = sketch + jnp.dot(onehot, mid, preferred_element_type=F32)
    sketch = sketch + jnp.dot(onehot, hi, preferred_element_type=F32)
    sk[...] = sketch
    save = lcopy(sk, sk_out, loc_sem.at[8])

    turned = jnp.transpose(sketch)

    def pieces(v):
        first = v.astype(BF16)
        v = v - first.astype(F32)
        second = v.astype(BF16)
        return first, second, (v - second.astype(F32)).astype(BF16)

    ta, tb, tc = pieces(turned)
    sa, sb, sc = pieces(sketch)
    gram = jnp.zeros((BPO, BPO), F32)
    for left, right in ((tc, sa), (ta, sc), (tb, sb), (tb, sa), (ta, sb), (ta, sa)):
        gram = gram + jnp.dot(left, right, preferred_element_type=F32)
    gp[pl.ds(0, 128), :] = gram[:HALF, :HALF]
    gp[pl.ds(128, 128), :] = gram[:HALF, HALF:]
    gp[pl.ds(256, 128), :] = gram[HALF:, HALF:]

    e = x * 2 + c
    near = [(d, dc) for d in (2, 1, 3, 0) for dc in range(2) if d or dc]
    got = []
    for d, dc in near:
        xt, ct = (x + d) % NX, (c + dc) % 2
        at = pl.ds((xt * 2 + ct) * 48, 48)
        got.append(rcopy(gp.at[at], gx.at[d * 2 + dc], x_s.at[d * 2 + dc], x_r.at[d * 2 + dc], dev(z, y, ct, xt)))
    total = gp[pl.ds(pl.multiple_of(e * 48, 8), 48), :]
    for (d, dc), cp in reversed(list(zip(near, got))):
        cp.wait_recv()
        total = total + gx[d * 2 + dc]
    acc[...] = total

    got = []
    for d in ORDER:
        zt = (z + d) % NZ
        got.append(rcopy(acc.at[pl.ds(zt * 6, 6)], gz.at[d, pl.ds(0, 6)], z_s.at[d], z_r.at[d], dev(zt, y, c, x)))
    total = acc[pl.ds(z * 6, 6), :]
    for d, cp in reversed(list(zip(ORDER, got))):
        cp.wait_recv()
        total = total + gz[d, 0:6]
    part[0:6, :] = total

    got = []
    for d in ORDER:
        yt = (y + d) % NY
        got.append(rcopy(part.at[pl.ds(0, 6)], gy.at[y, pl.ds(0, 6)], y_s.at[d], y_r.at[d], dev(z, yt, c, x)))
    gy[y, 0:6] = total
    for cp in got:
        cp.wait_recv()
    quad = [gy[2 * i, 0:6] + gy[2 * i + 1, 0:6] for i in range(4)]
    fin[pl.ds(z * 6, 6), :] = (quad[0] + quad[1]) + (quad[2] + quad[3])

    got = []
    mine = fin.at[pl.ds(z * 6, 6)]
    for d in ORDER:
        zt = (z + d) % NZ
        got.append(rcopy(mine, mine, zg_s.at[d], zg_r.at[d], dev(zt, y, c, x)))
    for cp in got:
        cp.wait_recv()

    got = []
    for d, dc in near:
        xt, ct = (x + d) % NX, (c + dc) % 2
        got.append(
            rcopy(fin, gfull.at[pl.ds(e * 48, 48)], xg_s.at[d * 2 + dc], xg_r.at[d * 2 + dc], dev(z, y, ct, xt))
        )
    gfull[pl.ds(pl.multiple_of(e * 48, 8), 48), :] = fin[...]
    for cp in got:
        cp.wait_recv()
    g_out[...] = gfull[...]
    save.wait()
    for cp in sends:
        cp.wait_send()


def splat(v):
    return jnp.broadcast_to(v, (8, HALF))


def recip(v):
    guess = pl.reciprocal(v, approx=True)
    return guess * (2.0 - v * guess)


def factor_block(mats, spread, turn, panels, put):
    for j in range(8):
        spread[j * 8:j * 8 + 8, :] = splat(mats[0][0:8, :][:, j:j + 1])
    for k in range(len(mats)):
        panels[k * 8:k * 8 + 8, :] = jnp.zeros((8, HALF), F32)
    index = lax.broadcasted_iota(jnp.int32, (HALF, HALF), 0)

    def step(p, carry):
        base = pl.multiple_of(p * 8, 8)
        back_by = lax.rem(HALF - base, HALF)
        d = [[spread[pl.ds(j * 8 + i, 8, stride=0), :] for j in range(i + 1)] for i in range(8)]
        rows = [[m[pl.ds(base + i, 8, stride=0), :] for m in mats] for i in range(8)]
        blocks = {1: [m[pl.ds(base + 8, 8), :] for m in mats]}
        rolled = pltpu.roll(blocks[1][0], back_by, 1)
        side = {1: [splat(rolled[:, j:j + 1]) for j in range(8)]}
        ahead = [splat(rolled[:, 8 + j:9 + j]) for j in range(8)]
        before = [panels[k * 8:k * 8 + 8, :] for k in range(len(mats))]
        for k, m in enumerate(mats):
            less = lax.dot_general(
                before[0], before[k], (((0,), (0,)), ((), ())),
                precision=lax.Precision.HIGHEST, preferred_element_type=F32,
            )
            m[0:HALF, :] = m[0:HALF, :] - jnp.where(index >= base + 16, less, 0.0)
        blocks[2] = [m[pl.ds(base + 16, 8), :] for m in mats]
        rolled = pltpu.roll(blocks[2][0], back_by, 1)
        side[2] = [splat(rolled[:, j:j + 1]) for j in range(8)]
        final = []
        for b in range(0, 8, 2):
            p00, p10, p11 = d[b][b], d[b + 1][b], d[b + 1][b + 1]
            inv = recip(p00 * p11 - p10 * p10)
            x0, x1 = rows[b], rows[b + 1]
            for g in (1, 2):
                v = side[g]
                n0 = p11 * v[b] - p10 * v[b + 1]
                n1 = p00 * v[b + 1] - p10 * v[b]
                blocks[g] = [t - (n0 * x0[k] + n1 * x1[k]) * inv for k, t in enumerate(blocks[g])]
                if g == 1:
                    to = b * 8
                    turn[to:to + 8, :] = v[b]
                    turn[to + 8:to + 16, :] = v[b + 1]
                    for j in range(8):
                        s0 = turn[pl.ds(to + j, 8, stride=0), :]
                        s1 = turn[pl.ds(to + 8 + j, 8, stride=0), :]
                        ahead[j] = ahead[j] - (n0 * s0 + n1 * s1) * inv
                if b < 6:
                    n0, n1 = n0 * inv, n1 * inv
                for i in range(b + 2, 8):
                    v[i] = v[i] - (n0 * d[i][b] + n1 * d[i][b + 1])
            for i in range(b + 2, 8):
                n0 = p11 * d[i][b] - p10 * d[i][b + 1]
                n1 = p00 * d[i][b + 1] - p10 * d[i][b]
                for j in range(b + 2, i + 1):
                    d[i][j] = d[i][j] - (n0 * d[j][b] + n1 * d[j][b + 1]) * inv
                n0, n1 = n0 * inv, n1 * inv
                rows[i] = [t - (n0 * x0[k] + n1 * x1[k]) for k, t in enumerate(rows[i])]
            r0 = lax.rsqrt(p00)
            low = p10 * r0
            r1 = lax.rsqrt(p11 - low * low)
            first = [t * r0 for t in x0]
            final.append(first)
            final.append([(t - low * first[k]) * r1 for k, t in enumerate(x1)])
        for j in range(8):
            spread[j * 8:j * 8 + 8, :] = ahead[j]
        for k, m in enumerate(mats):
            m[pl.ds(base + 8, 8), :] = blocks[1][k]
            m[pl.ds(base + 16, 8), :] = blocks[2][k]
            panel = jnp.concatenate([final[j][k][0:1, :] for j in range(8)], axis=0)
            panels[k * 8:k * 8 + 8, :] = panel
            put(base, k, panel)
        return carry

    lax.fori_loop(0, 16, step, 0)


def factor_kernel(scale, g_ref, sk_ref, f_out, sk_out, a0, a1, spread, turn, panels, sem):
    cp = pltpu.make_async_copy(sk_ref, sk_out, sem)
    cp.start()
    lane = lax.broadcasted_iota(jnp.int32, (8, HALF), 1)
    sub = lax.broadcasted_iota(jnp.int32, (8, HALF), 0)
    across, down = [], []
    for at in (0, 256):
        picked = [jnp.where(lane == sub + p * 8, g_ref[at + p * 8:at + p * 8 + 8, :], 0.0) for p in range(16)]
        down.append([lax.rsqrt(splat(jnp.sum(t, axis=1, keepdims=True))) for t in picked])
        while len(picked) > 1:
            picked = [picked[i] + picked[i + 1] for i in range(0, len(picked), 2)]
        across.append(splat(jnp.sum(picked[0], axis=0, keepdims=True)))
    scaled = [lax.rsqrt(v) for v in across]
    back = [jnp.sqrt(v * scale) for v in across]

    def put_at(first):
        def put(base, k, panel):
            panel = panel * back[first + k]
            if k == 0:
                panel = jnp.where(lane >= sub + base, panel, 0.0)
            lanes = slice((first + k) * HALF, (first + k + 1) * HALF)
            f_out[pl.ds(first * HALF + base, 8), lanes] = panel
        return put

    a0[HALF:HALF + 16, :] = jnp.zeros((16, HALF), F32)
    a1[HALF:HALF + 16, :] = jnp.zeros((16, HALF), F32)
    for p in range(16):
        at = p * 8
        a0[at:at + 8, :] = g_ref[at:at + 8, :] * (down[0][p] * scaled[0])
        a1[at:at + 8, :] = g_ref[128 + at:128 + at + 8, :] * (down[0][p] * scaled[1])
    f_out[128:256, 0:128] = jnp.zeros((128, 128), F32)
    factor_block([a0, a1], spread, turn, panels, put_at(0))
    corner = f_out[0:128, 128:256]
    less = lax.dot_general(
        corner, corner, (((0,), (0,)), ((), ())), precision=lax.Precision.HIGHEST, preferred_element_type=F32
    )
    for p in range(16):
        at = p * 8
        left = g_ref[256 + at:256 + at + 8, :] - less[at:at + 8, :] * (1.0 / scale)
        a0[at:at + 8, :] = left * (down[1][p] * scaled[1])
    factor_block([a0], spread, turn, panels, put_at(1))
    cp.wait()


def body(slab, buckets, signs, counts):
    owners = lax.axis_size("rows")
    capacity = slab.shape[1] // owners
    width = slab.shape[2]
    vm = pl.BlockSpec(memory_space=pltpu.VMEM)
    hbm = pl.BlockSpec(memory_space=pltpu.HBM)
    dma = pltpu.SemaphoreType.DMA
    sketch, gram = pl.pallas_call(
        gram_kernel,
        out_shape=(jax.ShapeDtypeStruct((BPO, width), F32), jax.ShapeDtypeStruct((384, 128), F32)),
        in_specs=[hbm] * 4,
        out_specs=(hbm, vm),
        scratch_shapes=[
            pltpu.VMEM((4, 2, 4, 2, 8, 256), F32),
            pltpu.VMEM((1, 512), jnp.int32),
            pltpu.VMEM((1, 512), jnp.int32),
            pltpu.VMEM((1, 128), jnp.int32),
            pltpu.VMEM((256, 256), F32),
            pltpu.VMEM((8, 128), jnp.int32),
            pltpu.VMEM((8, 2, 4, 8, 128), F32),
            pltpu.VMEM((8, 2, 4, 8, 128), F32),
            pltpu.VMEM((8, 8, 8, 128), F32),
            pltpu.VMEM((8, 8, 8, 128), F32),
            pltpu.VMEM((8, 128), jnp.int32),
            pltpu.VMEM((2, 8, 8, 128), jnp.int32),
            pltpu.VMEM((128, 128), jnp.int32),
            pltpu.VMEM((384, 128), F32),
            pltpu.VMEM((8, 48, 128), F32),
            pltpu.VMEM((48, 128), F32),
            pltpu.VMEM((8, 8, 128), F32),
            pltpu.VMEM((8, 128), F32),
            pltpu.VMEM((8, 8, 128), F32),
            pltpu.VMEM((48, 128), F32),
            pltpu.VMEM((384, 128), F32),
            dma((13,)),
            dma((16,)), dma((16,)), dma((16,)), dma((16,)), dma((8,)), dma((8,)),
            dma((16,)), dma((16,)), dma((16,)), dma((16,)), dma((16,)), dma((16,)),
            dma((8,)), dma((8,)), dma((8,)), dma((8,)), dma((8,)), dma((8,)),
            dma((8,)), dma((8,)), dma((8,)), dma((8,)),
        ],
        compiler_params=pltpu.CompilerParams(
            collective_id=0, has_side_effects=True, vmem_limit_bytes=60 * 1024 * 1024
        ),
    )(slab.reshape(4, 2, 4, 2, 8, width), buckets, signs, counts)
    slots = float(lax.axis_size("grp") * owners * owners * capacity)
    factor, sketch = pl.pallas_call(
        lambda *refs: factor_kernel(1.0 / slots, *refs),
        out_shape=(jax.ShapeDtypeStruct((width, width), F32), jax.ShapeDtypeStruct((BPO, width), F32)),
        in_specs=[vm, hbm],
        out_specs=(vm, hbm),
        scratch_shapes=[
            pltpu.VMEM((HALF + 16, HALF), F32),
            pltpu.VMEM((HALF + 16, HALF), F32),
            pltpu.VMEM((64, HALF), F32),
            pltpu.VMEM((64, HALF), F32),
            pltpu.VMEM((16, HALF), F32),
            pltpu.SemaphoreType.DMA,
        ],
        compiler_params=pltpu.CompilerParams(vmem_limit_bytes=60 * 1024 * 1024),
    )(gram, sketch)
    return (sketch.reshape(1, BPO, width), factor)


def solution(mesh):
    in_specs = (P("grp", "rows", None), P("grp", "rows"), P("grp", "rows"), P("grp", "rows"))
    out_specs = (P("grp", "rows", None), P())
    return jax.shard_map(body, mesh=mesh, in_specs=in_specs, out_specs=out_specs, check_vma=False)
```

```python
import jax
import jax.numpy as jnp
from jax import lax
from jax.experimental import pallas as pl
from jax.experimental.pallas import tpu as pltpu
from jax.sharding import PartitionSpec as P

NZ = 8
NY = 8
NX = 4
BPO = 256
HALF = 128
F32 = jnp.float32
BF16 = jnp.bfloat16
MESH = pl.DeviceIdType.MESH
ORDER = (4, 3, 5, 2, 6, 1, 7)


def gram_kernel(
    slab_hbm, buckets_hbm, signs_hbm, counts_hbm, sk_out, g_out,
    slab, buckets, signs, counts, sk, meta, r1a, r1b, r2a, r2b, m1, m2, mt, gp, gx, acc, gz, part, gy, fin, gfull,
    loc_sem, s1a_s, s1a_r, s1b_s, s1b_r, s1m_s, s1m_r, s2a_s, s2a_r, s2b_s, s2b_r, s2m_s, s2m_r,
    x_s, x_r, z_s, z_r, y_s, y_r, zg_s, zg_r, xg_s, xg_r,
):
    r = lax.axis_index("rows")
    x = lax.axis_index("grp")
    z = r // 16
    y = (r // 2) % 8
    c = r % 2

    def dev(zz, yy, cc, xx):
        return ((zz * NY + yy) * 2 + cc, xx)

    barrier = pltpu.get_barrier_semaphore()
    peers = [dev(z, y, 1 - c, x)]
    for d in range(1, 8):
        for dc in range(2):
            peers.append(dev((z + d) % NZ, y, (c + dc) % 2, x))
            peers.append(dev(z, (y + d) % NY, (c + dc) % 2, x))
    for d in range(1, 4):
        for dc in range(2):
            peers.append(dev(z, y, (c + dc) % 2, (x + d) % NX))
    for p in peers:
        pl.semaphore_signal(barrier, inc=1, device_id=p, device_id_type=MESH)

    sends = []

    def rcopy(src, dst, ss, rs, to):
        cp = pltpu.make_async_remote_copy(
            src_ref=src, dst_ref=dst, send_sem=ss, recv_sem=rs, device_id=to, device_id_type=MESH
        )
        cp.start()
        sends.append(cp)
        return cp

    def lcopy(src, dst, sem):
        cp = pltpu.make_async_copy(src, dst, sem)
        cp.start()
        return cp

    load = lcopy(slab_hbm, slab, loc_sem.at[2])
    small = [
        lcopy(counts_hbm, counts, loc_sem.at[5]),
        lcopy(signs_hbm, signs, loc_sem.at[6]),
        lcopy(buckets_hbm, buckets, loc_sem.at[7]),
    ]
    slot = lax.broadcasted_iota(jnp.int32, (HALF, 512), 1)
    pair = lax.broadcasted_iota(jnp.int32, (HALF, 512), 0)
    spread = jnp.where(slot // 4 == pair, 1.0, 0.0).astype(BF16)
    for cp in small:
        cp.wait()
    limit = jnp.dot(
        jnp.broadcast_to(counts[...], (8, HALF)).astype(F32).astype(BF16), spread, preferred_element_type=F32
    )[0:1, :]
    place = lax.broadcasted_iota(jnp.int32, (1, 512), 1) % 4
    weight = jnp.where(place.astype(F32) < limit, signs[...], 0)
    for t in range(NZ):
        meta[t:t + 1, 0:64] = buckets[0:1, t * 64:t * 64 + 64]
        meta[t:t + 1, 64:128] = weight[0:1, t * 64:t * 64 + 64]
    load.wait()
    own = {}
    for q in range(2):
        yl, zl = (y + q) % 2, (z + q) % 2
        own[q] = (
            lcopy(slab.at[z // 2, z % 2, :, yl, :, pl.ds(0, HALF)], r1a.at[z, yl], loc_sem.at[9 + q]),
            lcopy(slab.at[:, zl, y // 2, y % 2, :, pl.ds(HALF, HALF)], r1b.at[y, zl], loc_sem.at[11 + q]),
        )
    m1[pl.ds(z, 1), :] = meta[pl.ds(z, 1), :]
    pl.semaphore_wait(barrier, len(peers))

    in_m = []
    for d in ORDER:
        zt = (z + d) % NZ
        in_m.append(rcopy(meta.at[pl.ds(zt, 1)], m1.at[pl.ds(z, 1)], s1m_s.at[d], s1m_r.at[d], dev(zt, y, c, x)))
    in_a, in_b = {0: [], 1: []}, {0: [], 1: []}
    for q in (1, 0):
        yl, zl = (y + q) % 2, (z + q) % 2
        for d in ORDER:
            zt, yt = (z + d) % NZ, (y + d) % NY
            k = d * 2 + q
            in_a[q].append(rcopy(
                slab.at[zt // 2, zt % 2, :, yl, :, pl.ds(0, HALF)], r1a.at[z, yl],
                s1a_s.at[k], s1a_r.at[k], dev(zt, y, c, x),
            ))
            in_b[q].append(rcopy(
                slab.at[:, zl, yt // 2, yt % 2, :, pl.ds(HALF, HALF)], r1b.at[y, zl],
                s1b_s.at[k], s1b_r.at[k], dev(z, yt, c, x),
            ))

    for cp in in_m:
        cp.wait_recv()
    arrive = []
    for d in ORDER + (0,):
        for dc in range(2):
            if d == 0 and dc == 0:
                continue
            to = dev(z, (y + d) % NY, (c + dc) % 2, x)
            arrive.append(rcopy(m1, m2.at[c, y], s2m_s.at[d * 2 + dc], s2m_r.at[d * 2 + dc], to))
    m2[c, y] = m1[...]

    for q, order in ((1, (3, 5, 1, 7)), (0, (4, 2, 6, 0))):
        own[q][0].wait()
        for cp in in_a[q]:
            cp.wait_recv()
        for d in order:
            for dc in range(2):
                if d == 0 and dc == 0:
                    continue
                yt, ct, k = (y + d) % NY, (c + dc) % 2, d * 2 + dc
                arrive.append(rcopy(
                    r1a.at[:, yt % 2, yt // 2, pl.ds(ct * 4, 4), :], r2a.at[y, :, pl.ds(c * 4, 4), :],
                    s2a_s.at[k], s2a_r.at[k], dev(z, yt, ct, x),
                ))
        own[q][1].wait()
        for cp in in_b[q]:
            cp.wait_recv()
        for d in order:
            for dc in range(2):
                if d == 0 and dc == 0:
                    continue
                zt, ct, k = (z + d) % NZ, (c + dc) % 2, d * 2 + dc
                arrive.append(rcopy(
                    r1b.at[:, zt % 2, zt // 2, pl.ds(ct * 4, 4), :], r2b.at[:, z, pl.ds(c * 4, 4), :],
                    s2b_s.at[k], s2b_r.at[k], dev(zt, y, ct, x),
                ))
    l2a = lcopy(r1a.at[:, y % 2, y // 2, pl.ds(c * 4, 4), :], r2a.at[y, :, pl.ds(c * 4, 4), :], loc_sem.at[3])
    l2b = lcopy(r1b.at[:, z % 2, z // 2, pl.ds(c * 4, 4), :], r2b.at[:, z, pl.ds(c * 4, 4), :], loc_sem.at[4])

    n_m = 15
    for cp in arrive[:n_m]:
        cp.wait_recv()
    mt[...] = jnp.transpose(m2[...].reshape(128, 128))
    b4 = mt[pl.ds(y * 8 + c * 4, 4), :]
    w4 = mt[pl.ds(64 + y * 8 + c * 4, 4), :]
    row = lax.broadcasted_iota(jnp.int32, (BPO, 128), 0)
    onehot = jnp.concatenate(
        [jnp.where(row == b4[s:s + 1, :], w4[s:s + 1, :], 0).astype(F32) for s in range(4)], axis=1
    ).astype(BF16)

    for cp in arrive[n_m:]:
        cp.wait_recv()
    l2a.wait()
    l2b.wait()
    fa = r2a.reshape(512, 128)
    fb = r2b.reshape(512, 128)
    rows = jnp.concatenate(
        [
            jnp.concatenate([f[pl.ds(k * 4 + s, 64, stride=8), :] for s in range(4) for k in range(2)], axis=0)
            for f in (fa, fb)
        ],
        axis=1,
    )
    hi = rows.astype(BF16)
    rest = rows - hi.astype(F32)
    mid = rest.astype(BF16)
    low = (rest - mid.astype(F32)).astype(BF16)
    sketch = jnp.dot(onehot, low, preferred_element_type=F32)
    sketch = sketch + jnp.dot(onehot, mid, preferred_element_type=F32)
    sketch = sketch + jnp.dot(onehot, hi, preferred_element_type=F32)
    sk[...] = sketch
    save = lcopy(sk, sk_out, loc_sem.at[8])

    turned = jnp.transpose(sketch)

    def pieces(v):
        first = v.astype(BF16)
        v = v - first.astype(F32)
        second = v.astype(BF16)
        return first, second, (v - second.astype(F32)).astype(BF16)

    ta, tb, tc = pieces(turned)
    sa, sb, sc = pieces(sketch)
    gram = jnp.zeros((BPO, BPO), F32)
    for left, right in ((tc, sa), (ta, sc), (tb, sb), (tb, sa), (ta, sb), (ta, sa)):
        gram = gram + jnp.dot(left, right, preferred_element_type=F32)
    gp[pl.ds(0, 128), :] = gram[:HALF, :HALF]
    gp[pl.ds(128, 128), :] = gram[:HALF, HALF:]
    gp[pl.ds(256, 128), :] = gram[HALF:, HALF:]

    e = x * 2 + c
    near = [(d, dc) for d in (2, 1, 3, 0) for dc in range(2) if d or dc]
    got = []
    for d, dc in near:
        xt, ct = (x + d) % NX, (c + dc) % 2
        at = pl.ds((xt * 2 + ct) * 48, 48)
        got.append(rcopy(gp.at[at], gx.at[d * 2 + dc], x_s.at[d * 2 + dc], x_r.at[d * 2 + dc], dev(z, y, ct, xt)))
    total = gp[pl.ds(pl.multiple_of(e * 48, 8), 48), :]
    for (d, dc), cp in reversed(list(zip(near, got))):
        cp.wait_recv()
        total = total + gx[d * 2 + dc]
    acc[...] = total

    got = []
    for d in ORDER:
        zt = (z + d) % NZ
        got.append(rcopy(acc.at[pl.ds(zt * 6, 6)], gz.at[d, pl.ds(0, 6)], z_s.at[d], z_r.at[d], dev(zt, y, c, x)))
    total = acc[pl.ds(z * 6, 6), :]
    for d, cp in reversed(list(zip(ORDER, got))):
        cp.wait_recv()
        total = total + gz[d, 0:6]
    part[0:6, :] = total

    got = []
    for d in ORDER:
        yt = (y + d) % NY
        got.append(rcopy(part.at[pl.ds(0, 6)], gy.at[y, pl.ds(0, 6)], y_s.at[d], y_r.at[d], dev(z, yt, c, x)))
    gy[y, 0:6] = total
    for cp in got:
        cp.wait_recv()
    quad = [gy[2 * i, 0:6] + gy[2 * i + 1, 0:6] for i in range(4)]
    fin[pl.ds(z * 6, 6), :] = (quad[0] + quad[1]) + (quad[2] + quad[3])

    got = []
    mine = fin.at[pl.ds(z * 6, 6)]
    for d in ORDER:
        zt = (z + d) % NZ
        got.append(rcopy(mine, mine, zg_s.at[d], zg_r.at[d], dev(zt, y, c, x)))
    for cp in got:
        cp.wait_recv()

    got = []
    for d, dc in near:
        xt, ct = (x + d) % NX, (c + dc) % 2
        got.append(
            rcopy(fin, gfull.at[pl.ds(e * 48, 48)], xg_s.at[d * 2 + dc], xg_r.at[d * 2 + dc], dev(z, y, ct, xt))
        )
    gfull[pl.ds(pl.multiple_of(e * 48, 8), 48), :] = fin[...]
    for cp in got:
        cp.wait_recv()
    g_out[...] = gfull[...]
    save.wait()
    for cp in sends:
        cp.wait_send()


def splat(v):
    return jnp.broadcast_to(v, (8, HALF))


def recip(v):
    guess = pl.reciprocal(v, approx=True)
    return guess * (2.0 - v * guess)


def factor_block(mats, spread, turn, k0, emit):
    n = 16
    for p in range(n):
        base = p * 8
        at = (p % 2) * 64
        if p == 0:
            ahead = [splat(mats[0][0:8, :][:, j:j + 1]) for j in range(8)]
        for j in range(8):
            spread[at + j * 8:at + j * 8 + 8, :] = ahead[j]
        d = [[spread[pl.ds(at + j * 8 + i, 8, stride=0), :] for j in range(i + 1)] for i in range(8)]
        rows = [[m[pl.ds(base + i, 8, stride=0), :] for m in mats] for i in range(8)]
        near = list(range(p + 1, min(p + 4, n)))
        blocks = {g: [m[g * 8:g * 8 + 8, :] for m in mats] for g in near}
        side = {g: [splat(blocks[g][0][:, base + j:base + j + 1]) for j in range(8)] for g in near}
        if near:
            ahead = [splat(blocks[p + 1][0][:, base + 8 + j:base + 9 + j]) for j in range(8)]
        final = []
        for b in range(0, 8, 2):
            p00, p10, p11 = d[b][b], d[b + 1][b], d[b + 1][b + 1]
            inv = recip(p00 * p11 - p10 * p10)
            x0, x1 = rows[b], rows[b + 1]
            for g in near:
                v = side[g]
                n0 = p11 * v[b] - p10 * v[b + 1]
                n1 = p00 * v[b + 1] - p10 * v[b]
                blocks[g] = [t - (n0 * x0[k] + n1 * x1[k]) * inv for k, t in enumerate(blocks[g])]
                if g == p + 1:
                    to = at + b * 8
                    turn[to:to + 8, :] = v[b]
                    turn[to + 8:to + 16, :] = v[b + 1]
                    for j in range(8):
                        s0 = turn[pl.ds(to + j, 8, stride=0), :]
                        s1 = turn[pl.ds(to + 8 + j, 8, stride=0), :]
                        ahead[j] = ahead[j] - (n0 * s0 + n1 * s1) * inv
                if b < 6:
                    n0, n1 = n0 * inv, n1 * inv
                for i in range(b + 2, 8):
                    v[i] = v[i] - (n0 * d[i][b] + n1 * d[i][b + 1])
            for i in range(b + 2, 8):
                n0 = p11 * d[i][b] - p10 * d[i][b + 1]
                n1 = p00 * d[i][b + 1] - p10 * d[i][b]
                for j in range(b + 2, i + 1):
                    d[i][j] = d[i][j] - (n0 * d[j][b] + n1 * d[j][b + 1]) * inv
                n0, n1 = n0 * inv, n1 * inv
                rows[i] = [t - (n0 * x0[k] + n1 * x1[k]) for k, t in enumerate(rows[i])]
            r0 = lax.rsqrt(p00)
            low = p10 * r0
            r1 = lax.rsqrt(p11 - low * low)
            first = [t * r0 for t in x0]
            final.append(first)
            final.append([(t - low * first[k]) * r1 for k, t in enumerate(x1)])
        for g in near:
            for k, m in enumerate(mats):
                m[g * 8:g * 8 + 8, :] = blocks[g][k]
        for j in range(8):
            emit(k0 + base + j, base + j, [t[0:1, :] for t in final[j]])
        if p + 4 < n:
            first = (p + 4) * 8
            panel = [
                jnp.concatenate([final[j][k][0:1, :] for j in range(8)], axis=0) for k in range(len(mats))
            ]
            for k, m in enumerate(mats):
                less = lax.dot_general(
                    panel[0], panel[k], (((0,), (0,)), ((), ())),
                    precision=lax.Precision.HIGHEST, preferred_element_type=F32,
                )
                m[first:, :] = m[first:, :] - less[first:, :]


def factor_kernel(scale, g_ref, sk_ref, f_out, sk_out, a0, a1, spread, turn, sem):
    cp = pltpu.make_async_copy(sk_ref, sk_out, sem)
    cp.start()
    lane = lax.broadcasted_iota(jnp.int32, (8, HALF), 1)
    sub = lax.broadcasted_iota(jnp.int32, (8, HALF), 0)
    across, down = [], []
    for at in (0, 256):
        picked = [jnp.where(lane == sub + p * 8, g_ref[at + p * 8:at + p * 8 + 8, :], 0.0) for p in range(16)]
        down.append([lax.rsqrt(splat(jnp.sum(t, axis=1, keepdims=True))) for t in picked])
        while len(picked) > 1:
            picked = [picked[i] + picked[i + 1] for i in range(0, len(picked), 2)]
        across.append(splat(jnp.sum(picked[0], axis=0, keepdims=True)))
    scaled = [lax.rsqrt(v) for v in across]
    back = [jnp.sqrt(v * scale) for v in across]

    def emit(first):
        def put(at, diagonal, values):
            for k, v in enumerate(values):
                v = v * back[first + k][0:1, :]
                if k == 0:
                    v = jnp.where(lane[0:1, :] >= diagonal, v, 0.0)
                f_out[at:at + 1, (first + k) * HALF:(first + k + 1) * HALF] = v
        return put

    for p in range(16):
        at = p * 8
        a0[at:at + 8, :] = g_ref[at:at + 8, :] * (down[0][p] * scaled[0])
        a1[at:at + 8, :] = g_ref[128 + at:128 + at + 8, :] * (down[0][p] * scaled[1])
    f_out[128:256, 0:128] = jnp.zeros((128, 128), F32)
    factor_block([a0, a1], spread, turn, 0, emit(0))
    corner = f_out[0:128, 128:256]
    less = lax.dot_general(
        corner, corner, (((0,), (0,)), ((), ())), precision=lax.Precision.HIGHEST, preferred_element_type=F32
    )
    for p in range(16):
        at = p * 8
        left = g_ref[256 + at:256 + at + 8, :] - less[at:at + 8, :] * (1.0 / scale)
        a0[at:at + 8, :] = left * (down[1][p] * scaled[1])
    factor_block([a0], spread, turn, 128, emit(1))
    cp.wait()


def body(slab, buckets, signs, counts):
    owners = lax.axis_size("rows")
    capacity = slab.shape[1] // owners
    width = slab.shape[2]
    vm = pl.BlockSpec(memory_space=pltpu.VMEM)
    hbm = pl.BlockSpec(memory_space=pltpu.HBM)
    dma = pltpu.SemaphoreType.DMA
    sketch, gram = pl.pallas_call(
        gram_kernel,
        out_shape=(jax.ShapeDtypeStruct((BPO, width), F32), jax.ShapeDtypeStruct((384, 128), F32)),
        in_specs=[hbm] * 4,
        out_specs=(hbm, vm),
        scratch_shapes=[
            pltpu.VMEM((4, 2, 4, 2, 8, 256), F32),
            pltpu.VMEM((1, 512), jnp.int32),
            pltpu.VMEM((1, 512), jnp.int32),
            pltpu.VMEM((1, 128), jnp.int32),
            pltpu.VMEM((256, 256), F32),
            pltpu.VMEM((8, 128), jnp.int32),
            pltpu.VMEM((8, 2, 4, 8, 128), F32),
            pltpu.VMEM((8, 2, 4, 8, 128), F32),
            pltpu.VMEM((8, 8, 8, 128), F32),
            pltpu.VMEM((8, 8, 8, 128), F32),
            pltpu.VMEM((8, 128), jnp.int32),
            pltpu.VMEM((2, 8, 8, 128), jnp.int32),
            pltpu.VMEM((128, 128), jnp.int32),
            pltpu.VMEM((384, 128), F32),
            pltpu.VMEM((8, 48, 128), F32),
            pltpu.VMEM((48, 128), F32),
            pltpu.VMEM((8, 8, 128), F32),
            pltpu.VMEM((8, 128), F32),
            pltpu.VMEM((8, 8, 128), F32),
            pltpu.VMEM((48, 128), F32),
            pltpu.VMEM((384, 128), F32),
            dma((13,)),
            dma((16,)), dma((16,)), dma((16,)), dma((16,)), dma((8,)), dma((8,)),
            dma((16,)), dma((16,)), dma((16,)), dma((16,)), dma((16,)), dma((16,)),
            dma((8,)), dma((8,)), dma((8,)), dma((8,)), dma((8,)), dma((8,)),
            dma((8,)), dma((8,)), dma((8,)), dma((8,)),
        ],
        compiler_params=pltpu.CompilerParams(
            collective_id=0, has_side_effects=True, vmem_limit_bytes=60 * 1024 * 1024
        ),
    )(slab.reshape(4, 2, 4, 2, 8, width), buckets, signs, counts)
    slots = float(lax.axis_size("grp") * owners * owners * capacity)
    factor, sketch = pl.pallas_call(
        lambda *refs: factor_kernel(1.0 / slots, *refs),
        out_shape=(jax.ShapeDtypeStruct((width, width), F32), jax.ShapeDtypeStruct((BPO, width), F32)),
        in_specs=[vm, hbm],
        out_specs=(vm, hbm),
        scratch_shapes=[
            pltpu.VMEM((HALF, HALF), F32),
            pltpu.VMEM((HALF, HALF), F32),
            pltpu.VMEM((HALF, HALF), F32),
            pltpu.VMEM((HALF, HALF), F32),
            pltpu.SemaphoreType.DMA,
        ],
        compiler_params=pltpu.CompilerParams(vmem_limit_bytes=60 * 1024 * 1024),
    )(gram, sketch)
    return (sketch.reshape(1, BPO, width), factor)


def solution(mesh):
    in_specs = (P("grp", "rows", None), P("grp", "rows"), P("grp", "rows"), P("grp", "rows"))
    out_specs = (P("grp", "rows", None), P())
    return jax.shard_map(body, mesh=mesh, in_specs=in_specs, out_specs=out_specs, check_vma=False)
```

```python
import jax
import jax.numpy as jnp
from jax import lax
from jax.experimental import pallas as pl
from jax.experimental.pallas import tpu as pltpu
from jax.sharding import PartitionSpec as P

NZ = 8
NY = 8
NX = 4
BPO = 256
HALF = 128
F32 = jnp.float32
BF16 = jnp.bfloat16
MESH = pl.DeviceIdType.MESH
ORDER = (4, 3, 5, 2, 6, 1, 7)


def gram_kernel(
    slab_hbm, buckets_hbm, signs_hbm, counts_hbm, sk_out, g_out,
    slab, buckets, signs, counts, sk, meta, r1a, r1b, r2a, r2b, m1, m2, mt, gp, gc, gh, gx, acc, gz, part, gy, fin, gfull,
    loc_sem, s1a_s, s1a_r, s1b_s, s1b_r, s1m_s, s1m_r, s2a_s, s2a_r, s2b_s, s2b_r, s2m_s, s2m_r,
    x_s, x_r, z_s, z_r, y_s, y_r, zg_s, zg_r, xg_s, xg_r,
):
    r = lax.axis_index("rows")
    x = lax.axis_index("grp")
    z = r // 16
    y = (r // 2) % 8
    c = r % 2

    def dev(zz, yy, cc, xx):
        return ((zz * NY + yy) * 2 + cc, xx)

    barrier = pltpu.get_barrier_semaphore()
    peers = [dev(z, y, 1 - c, x)]
    for d in range(1, 8):
        for dc in range(2):
            peers.append(dev((z + d) % NZ, y, (c + dc) % 2, x))
            peers.append(dev(z, (y + d) % NY, (c + dc) % 2, x))
    for d in range(1, 4):
        for dc in range(2):
            peers.append(dev(z, y, (c + dc) % 2, (x + d) % NX))
    for p in peers:
        pl.semaphore_signal(barrier, inc=1, device_id=p, device_id_type=MESH)

    sends = []

    def rcopy(src, dst, ss, rs, to):
        cp = pltpu.make_async_remote_copy(
            src_ref=src, dst_ref=dst, send_sem=ss, recv_sem=rs, device_id=to, device_id_type=MESH
        )
        cp.start()
        sends.append(cp)
        return cp

    def lcopy(src, dst, sem):
        cp = pltpu.make_async_copy(src, dst, sem)
        cp.start()
        return cp

    load = lcopy(slab_hbm, slab, loc_sem.at[2])
    small = [
        lcopy(counts_hbm, counts, loc_sem.at[5]),
        lcopy(signs_hbm, signs, loc_sem.at[6]),
        lcopy(buckets_hbm, buckets, loc_sem.at[7]),
    ]
    slot = lax.broadcasted_iota(jnp.int32, (HALF, 512), 1)
    pair = lax.broadcasted_iota(jnp.int32, (HALF, 512), 0)
    spread = jnp.where(slot // 4 == pair, 1.0, 0.0).astype(BF16)
    for cp in small:
        cp.wait()
    limit = jnp.dot(
        jnp.broadcast_to(counts[...], (8, HALF)).astype(F32).astype(BF16), spread, preferred_element_type=F32
    )[0:1, :]
    place = lax.broadcasted_iota(jnp.int32, (1, 512), 1) % 4
    weight = jnp.where(place.astype(F32) < limit, signs[...], 0)
    for t in range(NZ):
        meta[t:t + 1, 0:64] = buckets[0:1, t * 64:t * 64 + 64]
        meta[t:t + 1, 64:128] = weight[0:1, t * 64:t * 64 + 64]
    load.wait()
    own = {}
    for q in range(2):
        yl, zl = (y + q) % 2, (z + q) % 2
        own[q] = (
            lcopy(slab.at[z // 2, z % 2, :, yl, :, pl.ds(0, HALF)], r1a.at[z, yl], loc_sem.at[9 + q]),
            lcopy(slab.at[:, zl, y // 2, y % 2, :, pl.ds(HALF, HALF)], r1b.at[y, zl], loc_sem.at[11 + q]),
        )
    m1[pl.ds(z, 1), :] = meta[pl.ds(z, 1), :]
    pl.semaphore_wait(barrier, len(peers))

    in_m = []
    for d in ORDER:
        zt = (z + d) % NZ
        in_m.append(rcopy(meta.at[pl.ds(zt, 1)], m1.at[pl.ds(z, 1)], s1m_s.at[d], s1m_r.at[d], dev(zt, y, c, x)))
    in_a, in_b = {0: [], 1: []}, {0: [], 1: []}
    for q in (1, 0):
        yl, zl = (y + q) % 2, (z + q) % 2
        for d in ORDER:
            zt, yt = (z + d) % NZ, (y + d) % NY
            k = d * 2 + q
            in_a[q].append(rcopy(
                slab.at[zt // 2, zt % 2, :, yl, :, pl.ds(0, HALF)], r1a.at[z, yl],
                s1a_s.at[k], s1a_r.at[k], dev(zt, y, c, x),
            ))
            in_b[q].append(rcopy(
                slab.at[:, zl, yt // 2, yt % 2, :, pl.ds(HALF, HALF)], r1b.at[y, zl],
                s1b_s.at[k], s1b_r.at[k], dev(z, yt, c, x),
            ))

    for cp in in_m:
        cp.wait_recv()
    arrive = []
    for d in ORDER + (0,):
        for dc in range(2):
            if d == 0 and dc == 0:
                continue
            to = dev(z, (y + d) % NY, (c + dc) % 2, x)
            arrive.append(rcopy(m1, m2.at[c, y], s2m_s.at[d * 2 + dc], s2m_r.at[d * 2 + dc], to))
    m2[c, y] = m1[...]

    for q, order in ((1, (3, 5, 1, 7)), (0, (4, 2, 6, 0))):
        own[q][0].wait()
        for cp in in_a[q]:
            cp.wait_recv()
        for d in order:
            for dc in range(2):
                if d == 0 and dc == 0:
                    continue
                yt, ct, k = (y + d) % NY, (c + dc) % 2, d * 2 + dc
                arrive.append(rcopy(
                    r1a.at[:, yt % 2, yt // 2, pl.ds(ct * 4, 4), :], r2a.at[y, :, pl.ds(c * 4, 4), :],
                    s2a_s.at[k], s2a_r.at[k], dev(z, yt, ct, x),
                ))
        own[q][1].wait()
        for cp in in_b[q]:
            cp.wait_recv()
        for d in order:
            for dc in range(2):
                if d == 0 and dc == 0:
                    continue
                zt, ct, k = (z + d) % NZ, (c + dc) % 2, d * 2 + dc
                arrive.append(rcopy(
                    r1b.at[:, zt % 2, zt // 2, pl.ds(ct * 4, 4), :], r2b.at[:, z, pl.ds(c * 4, 4), :],
                    s2b_s.at[k], s2b_r.at[k], dev(zt, y, ct, x),
                ))
    l2a = lcopy(r1a.at[:, y % 2, y // 2, pl.ds(c * 4, 4), :], r2a.at[y, :, pl.ds(c * 4, 4), :], loc_sem.at[3])
    l2b = lcopy(r1b.at[:, z % 2, z // 2, pl.ds(c * 4, 4), :], r2b.at[:, z, pl.ds(c * 4, 4), :], loc_sem.at[4])

    n_m = 15
    for cp in arrive[:n_m]:
        cp.wait_recv()
    mt[...] = jnp.transpose(m2[...].reshape(128, 128))
    b4 = mt[pl.ds(y * 8 + c * 4, 4), :]
    w4 = mt[pl.ds(64 + y * 8 + c * 4, 4), :]
    row = lax.broadcasted_iota(jnp.int32, (BPO, 128), 0)
    onehot = jnp.concatenate(
        [jnp.where(row == b4[s:s + 1, :], w4[s:s + 1, :], 0).astype(F32) for s in range(4)], axis=1
    ).astype(BF16)

    for cp in arrive[n_m:]:
        cp.wait_recv()
    l2a.wait()
    l2b.wait()
    fa = r2a.reshape(512, 128)
    fb = r2b.reshape(512, 128)
    rows = jnp.concatenate(
        [
            jnp.concatenate([f[pl.ds(k * 4 + s, 64, stride=8), :] for s in range(4) for k in range(2)], axis=0)
            for f in (fa, fb)
        ],
        axis=1,
    )
    hi = rows.astype(BF16)
    rest = rows - hi.astype(F32)
    mid = rest.astype(BF16)
    low = (rest - mid.astype(F32)).astype(BF16)
    sketch = jnp.dot(onehot, low, preferred_element_type=F32)
    sketch = sketch + jnp.dot(onehot, mid, preferred_element_type=F32)
    sketch = sketch + jnp.dot(onehot, hi, preferred_element_type=F32)
    sk[...] = sketch
    save = lcopy(sk, sk_out, loc_sem.at[8])

    turned = jnp.transpose(sketch)

    def pieces(v):
        first = v.astype(BF16)
        v = v - first.astype(F32)
        second = v.astype(BF16)
        return first, second, (v - second.astype(F32)).astype(BF16)

    ta, tb, tc = pieces(turned)
    sa, sb, sc = pieces(sketch)
    gram = jnp.zeros((BPO, BPO), F32)
    for left, right in ((tc, sa), (ta, sc), (tb, sb), (tb, sa), (ta, sb), (ta, sa)):
        gram = gram + jnp.dot(left, right, preferred_element_type=F32)
    gp[pl.ds(0, 128), :] = gram[:HALF, :HALF]
    gp[pl.ds(128, 128), :] = gram[:HALF, HALF:]
    gp[pl.ds(256, 128), :] = gram[HALF:, HALF:]

    e = x * 2 + c
    sibling = dev(z, y, 1 - c, x)
    quarters = gp.reshape(4, 96, 128)
    rcopy(quarters.at[:, pl.ds((1 - c) * 48, 48)], gc, x_s.at[0], x_r.at[0], sibling).wait_recv()
    for i in range(4):
        gh[i] = gp[pl.ds(pl.multiple_of(i * 96 + c * 48, 8), 48), :] + gc[i]
    got = []
    for d in (2, 1, 3):
        xt = (x + d) % NX
        got.append(rcopy(gh.at[xt], gx.at[d], x_s.at[d], x_r.at[d], dev(z, y, c, xt)))
    total = gh[x]
    for d, cp in reversed(list(zip((2, 1, 3), got))):
        cp.wait_recv()
        total = total + gx[d]
    acc[...] = total

    got = []
    for d in ORDER:
        zt = (z + d) % NZ
        got.append(rcopy(acc.at[pl.ds(zt * 6, 6)], gz.at[d, pl.ds(0, 6)], z_s.at[d], z_r.at[d], dev(zt, y, c, x)))
    total = acc[pl.ds(z * 6, 6), :]
    for d, cp in reversed(list(zip(ORDER, got))):
        cp.wait_recv()
        total = total + gz[d, 0:6]
    part[0:6, :] = total

    got = []
    for d in ORDER:
        yt = (y + d) % NY
        got.append(rcopy(part.at[pl.ds(0, 6)], gy.at[y, pl.ds(0, 6)], y_s.at[d], y_r.at[d], dev(z, yt, c, x)))
    gy[y, 0:6] = total
    for cp in got:
        cp.wait_recv()
    quad = [gy[2 * i, 0:6] + gy[2 * i + 1, 0:6] for i in range(4)]
    fin[pl.ds(z * 6, 6), :] = (quad[0] + quad[1]) + (quad[2] + quad[3])

    got = []
    mine = fin.at[pl.ds(z * 6, 6)]
    for d in ORDER:
        zt = (z + d) % NZ
        got.append(rcopy(mine, mine, zg_s.at[d], zg_r.at[d], dev(zt, y, c, x)))
    for cp in got:
        cp.wait_recv()

    def place_of(xx):
        return gfull.at[pl.ds((xx * 2 + c) * 48, 48)]

    got = []
    for d in (2, 1, 3):
        xt = (x + d) % NX
        got.append(rcopy(fin, place_of(x), xg_s.at[d], xg_r.at[d], dev(z, y, c, xt)))
    over = [rcopy(fin, place_of(x), xg_s.at[4], xg_r.at[4], sibling)]
    gfull[pl.ds(pl.multiple_of(e * 48, 8), 48), :] = fin[...]
    for d, cp in reversed(list(zip((2, 1, 3), got))):
        cp.wait_recv()
        piece = place_of((x + NX - d) % NX)
        over.append(rcopy(piece, piece, xg_s.at[4 + d], xg_r.at[4 + d], sibling))
    for cp in over:
        cp.wait_recv()
    g_out[...] = gfull[...]
    save.wait()
    for cp in sends:
        cp.wait_send()


def splat(v):
    return jnp.broadcast_to(v, (8, HALF))


def recip(v):
    guess = pl.reciprocal(v, approx=True)
    return guess * (2.0 - v * guess)


def factor_block(mats, spread, k0, emit):
    n = 16
    for p in range(n):
        base = p * 8
        lead = mats[0][base:base + 8, :]
        at = (p % 2) * 64
        for j in range(8):
            spread[at + j * 8:at + j * 8 + 8, :] = splat(lead[:, base + j:base + j + 1])
        d = [[spread[pl.ds(at + j * 8 + i, 8, stride=0), :] for j in range(i + 1)] for i in range(8)]
        rows = [[m[pl.ds(base + i, 8, stride=0), :] for m in mats] for i in range(8)]
        near = list(range(p + 1, min(p + 3, n)))
        blocks = {g: [m[g * 8:g * 8 + 8, :] for m in mats] for g in near}
        side = {g: [splat(blocks[g][0][:, base + j:base + j + 1]) for j in range(8)] for g in near}
        final = []
        for b in range(0, 8, 2):
            p00, p10, p11 = d[b][b], d[b + 1][b], d[b + 1][b + 1]
            inv = recip(p00 * p11 - p10 * p10)
            x0, x1 = rows[b], rows[b + 1]
            for g in near:
                v = side[g]
                n0 = p11 * v[b] - p10 * v[b + 1]
                n1 = p00 * v[b + 1] - p10 * v[b]
                blocks[g] = [t - (n0 * x0[k] + n1 * x1[k]) * inv for k, t in enumerate(blocks[g])]
                if b < 6:
                    n0, n1 = n0 * inv, n1 * inv
                for i in range(b + 2, 8):
                    v[i] = v[i] - (n0 * d[i][b] + n1 * d[i][b + 1])
            for i in range(b + 2, 8):
                n0 = p11 * d[i][b] - p10 * d[i][b + 1]
                n1 = p00 * d[i][b + 1] - p10 * d[i][b]
                for j in range(b + 2, i + 1):
                    d[i][j] = d[i][j] - (n0 * d[j][b] + n1 * d[j][b + 1]) * inv
                n0, n1 = n0 * inv, n1 * inv
                rows[i] = [t - (n0 * x0[k] + n1 * x1[k]) for k, t in enumerate(rows[i])]
            r0 = lax.rsqrt(p00)
            low = p10 * r0
            r1 = lax.rsqrt(p11 - low * low)
            first = [t * r0 for t in x0]
            final.append(first)
            final.append([(t - low * first[k]) * r1 for k, t in enumerate(x1)])
        for g in near:
            for k, m in enumerate(mats):
                m[g * 8:g * 8 + 8, :] = blocks[g][k]
        for j in range(8):
            emit(k0 + base + j, base + j, [t[0:1, :] for t in final[j]])
        if p + 3 < n:
            first = (p + 3) * 8
            panel = [
                jnp.concatenate([final[j][k][0:1, :] for j in range(8)], axis=0) for k in range(len(mats))
            ]
            for k, m in enumerate(mats):
                less = lax.dot_general(
                    panel[0], panel[k], (((0,), (0,)), ((), ())),
                    precision=lax.Precision.HIGHEST, preferred_element_type=F32,
                )
                m[first:, :] = m[first:, :] - less[first:, :]


def factor_kernel(scale, g_ref, sk_ref, f_out, sk_out, a0, a1, spread, sem):
    cp = pltpu.make_async_copy(sk_ref, sk_out, sem)
    cp.start()
    lane = lax.broadcasted_iota(jnp.int32, (8, HALF), 1)
    sub = lax.broadcasted_iota(jnp.int32, (8, HALF), 0)
    across, down = [], []
    for at in (0, 256):
        picked = [jnp.where(lane == sub + p * 8, g_ref[at + p * 8:at + p * 8 + 8, :], 0.0) for p in range(16)]
        down.append([lax.rsqrt(splat(jnp.sum(t, axis=1, keepdims=True))) for t in picked])
        while len(picked) > 1:
            picked = [picked[i] + picked[i + 1] for i in range(0, len(picked), 2)]
        across.append(splat(jnp.sum(picked[0], axis=0, keepdims=True)))
    scaled = [lax.rsqrt(v) for v in across]
    back = [jnp.sqrt(v * scale) for v in across]

    def emit(first):
        def put(at, diagonal, values):
            for k, v in enumerate(values):
                v = v * back[first + k][0:1, :]
                if k == 0:
                    v = jnp.where(lane[0:1, :] >= diagonal, v, 0.0)
                f_out[at:at + 1, (first + k) * HALF:(first + k + 1) * HALF] = v
        return put

    for p in range(16):
        at = p * 8
        a0[at:at + 8, :] = g_ref[at:at + 8, :] * (down[0][p] * scaled[0])
        a1[at:at + 8, :] = g_ref[128 + at:128 + at + 8, :] * (down[0][p] * scaled[1])
    f_out[128:256, 0:128] = jnp.zeros((128, 128), F32)
    factor_block([a0, a1], spread, 0, emit(0))
    corner = f_out[0:128, 128:256]
    less = lax.dot_general(
        corner, corner, (((0,), (0,)), ((), ())), precision=lax.Precision.HIGHEST, preferred_element_type=F32
    )
    for p in range(16):
        at = p * 8
        left = g_ref[256 + at:256 + at + 8, :] - less[at:at + 8, :] * (1.0 / scale)
        a0[at:at + 8, :] = left * (down[1][p] * scaled[1])
    factor_block([a0], spread, 128, emit(1))
    cp.wait()


def body(slab, buckets, signs, counts):
    owners = lax.axis_size("rows")
    capacity = slab.shape[1] // owners
    width = slab.shape[2]
    vm = pl.BlockSpec(memory_space=pltpu.VMEM)
    hbm = pl.BlockSpec(memory_space=pltpu.HBM)
    dma = pltpu.SemaphoreType.DMA
    sketch, gram = pl.pallas_call(
        gram_kernel,
        out_shape=(jax.ShapeDtypeStruct((BPO, width), F32), jax.ShapeDtypeStruct((384, 128), F32)),
        in_specs=[hbm] * 4,
        out_specs=(hbm, vm),
        scratch_shapes=[
            pltpu.VMEM((4, 2, 4, 2, 8, 256), F32),
            pltpu.VMEM((1, 512), jnp.int32),
            pltpu.VMEM((1, 512), jnp.int32),
            pltpu.VMEM((1, 128), jnp.int32),
            pltpu.VMEM((256, 256), F32),
            pltpu.VMEM((8, 128), jnp.int32),
            pltpu.VMEM((8, 2, 4, 8, 128), F32),
            pltpu.VMEM((8, 2, 4, 8, 128), F32),
            pltpu.VMEM((8, 8, 8, 128), F32),
            pltpu.VMEM((8, 8, 8, 128), F32),
            pltpu.VMEM((8, 128), jnp.int32),
            pltpu.VMEM((2, 8, 8, 128), jnp.int32),
            pltpu.VMEM((128, 128), jnp.int32),
            pltpu.VMEM((384, 128), F32),
            pltpu.VMEM((4, 48, 128), F32),
            pltpu.VMEM((4, 48, 128), F32),
            pltpu.VMEM((8, 48, 128), F32),
            pltpu.VMEM((48, 128), F32),
            pltpu.VMEM((8, 8, 128), F32),
            pltpu.VMEM((8, 128), F32),
            pltpu.VMEM((8, 8, 128), F32),
            pltpu.VMEM((48, 128), F32),
            pltpu.VMEM((384, 128), F32),
            dma((13,)),
            dma((16,)), dma((16,)), dma((16,)), dma((16,)), dma((8,)), dma((8,)),
            dma((16,)), dma((16,)), dma((16,)), dma((16,)), dma((16,)), dma((16,)),
            dma((8,)), dma((8,)), dma((8,)), dma((8,)), dma((8,)), dma((8,)),
            dma((8,)), dma((8,)), dma((8,)), dma((8,)),
        ],
        compiler_params=pltpu.CompilerParams(
            collective_id=0, has_side_effects=True, vmem_limit_bytes=60 * 1024 * 1024
        ),
    )(slab.reshape(4, 2, 4, 2, 8, width), buckets, signs, counts)
    slots = float(lax.axis_size("grp") * owners * owners * capacity)
    factor, sketch = pl.pallas_call(
        lambda *refs: factor_kernel(1.0 / slots, *refs),
        out_shape=(jax.ShapeDtypeStruct((width, width), F32), jax.ShapeDtypeStruct((BPO, width), F32)),
        in_specs=[vm, hbm],
        out_specs=(vm, hbm),
        scratch_shapes=[
            pltpu.VMEM((HALF, HALF), F32),
            pltpu.VMEM((HALF, HALF), F32),
            pltpu.VMEM((HALF, HALF), F32),
            pltpu.SemaphoreType.DMA,
        ],
        compiler_params=pltpu.CompilerParams(vmem_limit_bytes=60 * 1024 * 1024),
    )(gram, sketch)
    return (sketch.reshape(1, BPO, width), factor)


def solution(mesh):
    in_specs = (P("grp", "rows", None), P("grp", "rows"), P("grp", "rows"), P("grp", "rows"))
    out_specs = (P("grp", "rows", None), P())
    return jax.shard_map(body, mesh=mesh, in_specs=in_specs, out_specs=out_specs, check_vma=False)
```

```python
import jax
import jax.numpy as jnp
from jax import lax
from jax.experimental import pallas as pl
from jax.experimental.pallas import tpu as pltpu
from jax.sharding import PartitionSpec as P

NZ = 8
NY = 8
NX = 4
BPO = 256
HALF = 128
F32 = jnp.float32
BF16 = jnp.bfloat16
MESH = pl.DeviceIdType.MESH
ORDER = (4, 3, 5, 2, 6, 1, 7)


def gram_kernel(
    slab_hbm, buckets_hbm, signs_hbm, counts_hbm, sk_out, g_out,
    slab, buckets, signs, counts, sk, meta, r1a, r1b, r2a, r2b, m1, m2, mt, gp, gx, acc, gz, part, gy, fin, gfull,
    loc_sem, s1a_s, s1a_r, s1b_s, s1b_r, s1m_s, s1m_r, s2a_s, s2a_r, s2b_s, s2b_r, s2m_s, s2m_r,
    x_s, x_r, z_s, z_r, y_s, y_r, zg_s, zg_r, xg_s, xg_r,
):
    r = lax.axis_index("rows")
    x = lax.axis_index("grp")
    z = r // 16
    y = (r // 2) % 8
    c = r % 2

    def dev(zz, yy, cc, xx):
        return ((zz * NY + yy) * 2 + cc, xx)

    barrier = pltpu.get_barrier_semaphore()
    peers = [dev(z, y, 1 - c, x)]
    for d in range(1, 8):
        for dc in range(2):
            peers.append(dev((z + d) % NZ, y, (c + dc) % 2, x))
            peers.append(dev(z, (y + d) % NY, (c + dc) % 2, x))
    for d in range(1, 4):
        for dc in range(2):
            peers.append(dev(z, y, (c + dc) % 2, (x + d) % NX))
    def lcopy(src, dst, sem):
        cp = pltpu.make_async_copy(src, dst, sem)
        cp.start()
        return cp

    load = lcopy(slab_hbm, slab, loc_sem.at[2])
    small = [
        lcopy(counts_hbm, counts, loc_sem.at[5]),
        lcopy(signs_hbm, signs, loc_sem.at[6]),
        lcopy(buckets_hbm, buckets, loc_sem.at[7]),
    ]
    for p in peers:
        pl.semaphore_signal(barrier, inc=1, device_id=p, device_id_type=MESH)

    sends = []

    def rcopy(src, dst, ss, rs, to):
        cp = pltpu.make_async_remote_copy(
            src_ref=src, dst_ref=dst, send_sem=ss, recv_sem=rs, device_id=to, device_id_type=MESH
        )
        cp.start()
        sends.append(cp)
        return cp

    slot = lax.broadcasted_iota(jnp.int32, (HALF, 512), 1)
    pair = lax.broadcasted_iota(jnp.int32, (HALF, 512), 0)
    spread = jnp.where(slot // 4 == pair, 1.0, 0.0).astype(BF16)
    for cp in small:
        cp.wait()
    limit = jnp.dot(
        jnp.broadcast_to(counts[...], (8, HALF)).astype(F32).astype(BF16), spread, preferred_element_type=F32
    )[0:1, :]
    place = lax.broadcasted_iota(jnp.int32, (1, 512), 1) % 4
    weight = jnp.where(place.astype(F32) < limit, signs[...], 0)
    for t in range(NZ):
        meta[t:t + 1, 0:64] = buckets[0:1, t * 64:t * 64 + 64]
        meta[t:t + 1, 64:128] = weight[0:1, t * 64:t * 64 + 64]
    load.wait()
    own = {}
    for q in range(2):
        yl, zl = (y + q) % 2, (z + q) % 2
        own[q] = (
            lcopy(slab.at[z // 2, z % 2, :, yl, :, pl.ds(0, HALF)], r1a.at[z, yl], loc_sem.at[9 + q]),
            lcopy(slab.at[:, zl, y // 2, y % 2, :, pl.ds(HALF, HALF)], r1b.at[y, zl], loc_sem.at[11 + q]),
        )
    m1[pl.ds(z, 1), :] = meta[pl.ds(z, 1), :]
    pl.semaphore_wait(barrier, len(peers))

    in_m = []
    for d in ORDER:
        zt = (z + d) % NZ
        in_m.append(rcopy(meta.at[pl.ds(zt, 1)], m1.at[pl.ds(z, 1)], s1m_s.at[d], s1m_r.at[d], dev(zt, y, c, x)))
    in_a, in_b = {0: [], 1: []}, {0: [], 1: []}
    for q in (1, 0):
        yl, zl = (y + q) % 2, (z + q) % 2
        for d in ORDER:
            zt, yt = (z + d) % NZ, (y + d) % NY
            k = d * 2 + q
            in_a[q].append(rcopy(
                slab.at[zt // 2, zt % 2, :, yl, :, pl.ds(0, HALF)], r1a.at[z, yl],
                s1a_s.at[k], s1a_r.at[k], dev(zt, y, c, x),
            ))
            in_b[q].append(rcopy(
                slab.at[:, zl, yt // 2, yt % 2, :, pl.ds(HALF, HALF)], r1b.at[y, zl],
                s1b_s.at[k], s1b_r.at[k], dev(z, yt, c, x),
            ))

    for cp in in_m:
        cp.wait_recv()
    arrive = []
    for d in ORDER + (0,):
        for dc in range(2):
            if d == 0 and dc == 0:
                continue
            to = dev(z, (y + d) % NY, (c + dc) % 2, x)
            arrive.append(rcopy(m1, m2.at[c, y], s2m_s.at[d * 2 + dc], s2m_r.at[d * 2 + dc], to))
    m2[c, y] = m1[...]

    for q, order in ((1, (3, 5, 1, 7)), (0, (4, 2, 6, 0))):
        own[q][0].wait()
        for cp in in_a[q]:
            cp.wait_recv()
        for d in order:
            for dc in range(2):
                if d == 0 and dc == 0:
                    continue
                yt, ct, k = (y + d) % NY, (c + dc) % 2, d * 2 + dc
                arrive.append(rcopy(
                    r1a.at[:, yt % 2, yt // 2, pl.ds(ct * 4, 4), :], r2a.at[y, :, pl.ds(c * 4, 4), :],
                    s2a_s.at[k], s2a_r.at[k], dev(z, yt, ct, x),
                ))
        own[q][1].wait()
        for cp in in_b[q]:
            cp.wait_recv()
        for d in order:
            for dc in range(2):
                if d == 0 and dc == 0:
                    continue
                zt, ct, k = (z + d) % NZ, (c + dc) % 2, d * 2 + dc
                arrive.append(rcopy(
                    r1b.at[:, zt % 2, zt // 2, pl.ds(ct * 4, 4), :], r2b.at[:, z, pl.ds(c * 4, 4), :],
                    s2b_s.at[k], s2b_r.at[k], dev(zt, y, ct, x),
                ))
    l2a = lcopy(r1a.at[:, y % 2, y // 2, pl.ds(c * 4, 4), :], r2a.at[y, :, pl.ds(c * 4, 4), :], loc_sem.at[3])
    l2b = lcopy(r1b.at[:, z % 2, z // 2, pl.ds(c * 4, 4), :], r2b.at[:, z, pl.ds(c * 4, 4), :], loc_sem.at[4])

    n_m = 15
    for cp in arrive[:n_m]:
        cp.wait_recv()
    mt[...] = jnp.transpose(m2[...].reshape(128, 128))
    b4 = mt[pl.ds(y * 8 + c * 4, 4), :]
    w4 = mt[pl.ds(64 + y * 8 + c * 4, 4), :]
    row = lax.broadcasted_iota(jnp.int32, (BPO, 128), 0)
    onehot = jnp.concatenate(
        [jnp.where(row == b4[s:s + 1, :], w4[s:s + 1, :], 0).astype(F32) for s in range(4)], axis=1
    ).astype(BF16)

    for cp in arrive[n_m:]:
        cp.wait_recv()
    l2a.wait()
    l2b.wait()
    fa = r2a.reshape(512, 128)
    fb = r2b.reshape(512, 128)
    rows = jnp.concatenate(
        [
            jnp.concatenate([f[pl.ds(k * 4 + s, 64, stride=8), :] for s in range(4) for k in range(2)], axis=0)
            for f in (fa, fb)
        ],
        axis=1,
    )
    hi = rows.astype(BF16)
    rest = rows - hi.astype(F32)
    mid = rest.astype(BF16)
    low = (rest - mid.astype(F32)).astype(BF16)
    sketch = jnp.dot(onehot, low, preferred_element_type=F32)
    sketch = sketch + jnp.dot(onehot, mid, preferred_element_type=F32)
    sketch = sketch + jnp.dot(onehot, hi, preferred_element_type=F32)
    sk[...] = sketch
    save = lcopy(sk, sk_out, loc_sem.at[8])

    turned = jnp.transpose(sketch)

    def pieces(v):
        first = v.astype(BF16)
        v = v - first.astype(F32)
        second = v.astype(BF16)
        return first, second, (v - second.astype(F32)).astype(BF16)

    ta, tb, tc = pieces(turned)
    sa, sb, sc = pieces(sketch)
    gram = jnp.zeros((BPO, BPO), F32)
    for left, right in ((tc, sa), (ta, sc), (tb, sb), (tb, sa), (ta, sb), (ta, sa)):
        gram = gram + jnp.dot(left, right, preferred_element_type=F32)
    gp[pl.ds(0, 128), :] = gram[:HALF, :HALF]
    gp[pl.ds(128, 128), :] = gram[:HALF, HALF:]
    gp[pl.ds(256, 128), :] = gram[HALF:, HALF:]

    e = x * 2 + c
    near = [(d, dc) for d in (2, 1, 3, 0) for dc in range(2) if d or dc]
    got = []
    for d, dc in near:
        xt, ct = (x + d) % NX, (c + dc) % 2
        at = pl.ds((xt * 2 + ct) * 48, 48)
        got.append(rcopy(gp.at[at], gx.at[d * 2 + dc], x_s.at[d * 2 + dc], x_r.at[d * 2 + dc], dev(z, y, ct, xt)))
    total = gp[pl.ds(pl.multiple_of(e * 48, 8), 48), :]
    for (d, dc), cp in reversed(list(zip(near, got))):
        cp.wait_recv()
        total = total + gx[d * 2 + dc]
    acc[...] = total

    got = []
    for d in ORDER:
        zt = (z + d) % NZ
        got.append(rcopy(acc.at[pl.ds(zt * 6, 6)], gz.at[d, pl.ds(0, 6)], z_s.at[d], z_r.at[d], dev(zt, y, c, x)))
    total = acc[pl.ds(z * 6, 6), :]
    for d, cp in reversed(list(zip(ORDER, got))):
        cp.wait_recv()
        total = total + gz[d, 0:6]
    part[0:6, :] = total

    got = []
    for d in ORDER:
        yt = (y + d) % NY
        got.append(rcopy(part.at[pl.ds(0, 6)], gy.at[y, pl.ds(0, 6)], y_s.at[d], y_r.at[d], dev(z, yt, c, x)))
    gy[y, 0:6] = total
    for cp in got:
        cp.wait_recv()
    quad = [gy[2 * i, 0:6] + gy[2 * i + 1, 0:6] for i in range(4)]
    fin[pl.ds(z * 6, 6), :] = (quad[0] + quad[1]) + (quad[2] + quad[3])

    got = []
    mine = fin.at[pl.ds(z * 6, 6)]
    for d in ORDER:
        zt = (z + d) % NZ
        got.append(rcopy(mine, mine, zg_s.at[d], zg_r.at[d], dev(zt, y, c, x)))
    for cp in got:
        cp.wait_recv()

    got = []
    for d, dc in near:
        xt, ct = (x + d) % NX, (c + dc) % 2
        got.append(
            rcopy(fin, gfull.at[pl.ds(e * 48, 48)], xg_s.at[d * 2 + dc], xg_r.at[d * 2 + dc], dev(z, y, ct, xt))
        )
    gfull[pl.ds(pl.multiple_of(e * 48, 8), 48), :] = fin[...]
    for cp in got:
        cp.wait_recv()
    g_out[...] = gfull[...]
    save.wait()
    for cp in sends:
        cp.wait_send()


def splat(v):
    return jnp.broadcast_to(v, (8, HALF))


def recip(v):
    guess = pl.reciprocal(v, approx=True)
    return guess * (2.0 - v * guess)


def factor_block(mats, spread, k0, emit):
    n = 16
    for p in range(n):
        base = p * 8
        lead = mats[0][base:base + 8, :]
        at = (p % 2) * 64
        for j in range(8):
            spread[at + j * 8:at + j * 8 + 8, :] = splat(lead[:, base + j:base + j + 1])
        d = [[spread[pl.ds(at + j * 8 + i, 8, stride=0), :] for j in range(i + 1)] for i in range(8)]
        rows = [[m[pl.ds(base + i, 8, stride=0), :] for m in mats] for i in range(8)]
        near = list(range(p + 1, min(p + 3, n)))
        blocks = {g: [m[g * 8:g * 8 + 8, :] for m in mats] for g in near}
        side = {g: [splat(blocks[g][0][:, base + j:base + j + 1]) for j in range(8)] for g in near}
        final = []
        for b in range(0, 8, 2):
            p00, p10, p11 = d[b][b], d[b + 1][b], d[b + 1][b + 1]
            inv = recip(p00 * p11 - p10 * p10)
            x0, x1 = rows[b], rows[b + 1]
            for g in near:
                v = side[g]
                n0 = p11 * v[b] - p10 * v[b + 1]
                n1 = p00 * v[b + 1] - p10 * v[b]
                blocks[g] = [t - (n0 * x0[k] + n1 * x1[k]) * inv for k, t in enumerate(blocks[g])]
                if b < 6:
                    n0, n1 = n0 * inv, n1 * inv
                for i in range(b + 2, 8):
                    v[i] = v[i] - (n0 * d[i][b] + n1 * d[i][b + 1])
            for i in range(b + 2, 8):
                n0 = p11 * d[i][b] - p10 * d[i][b + 1]
                n1 = p00 * d[i][b + 1] - p10 * d[i][b]
                for j in range(b + 2, i + 1):
                    d[i][j] = d[i][j] - (n0 * d[j][b] + n1 * d[j][b + 1]) * inv
                n0, n1 = n0 * inv, n1 * inv
                rows[i] = [t - (n0 * x0[k] + n1 * x1[k]) for k, t in enumerate(rows[i])]
            r0 = lax.rsqrt(p00)
            low = p10 * r0
            r1 = lax.rsqrt(p11 - low * low)
            first = [t * r0 for t in x0]
            final.append(first)
            final.append([(t - low * first[k]) * r1 for k, t in enumerate(x1)])
        for g in near:
            for k, m in enumerate(mats):
                m[g * 8:g * 8 + 8, :] = blocks[g][k]
        for j in range(8):
            emit(k0 + base + j, base + j, [t[0:1, :] for t in final[j]])
        if p + 3 < n:
            first = (p + 3) * 8
            panel = [
                jnp.concatenate([final[j][k][0:1, :] for j in range(8)], axis=0) for k in range(len(mats))
            ]
            for k, m in enumerate(mats):
                less = lax.dot_general(
                    panel[0], panel[k], (((0,), (0,)), ((), ())),
                    precision=lax.Precision.HIGHEST, preferred_element_type=F32,
                )
                m[first:, :] = m[first:, :] - less[first:, :]


def factor_kernel(scale, g_ref, sk_ref, f_out, sk_out, a0, a1, spread, sem):
    cp = pltpu.make_async_copy(sk_ref, sk_out, sem)
    cp.start()
    lane = lax.broadcasted_iota(jnp.int32, (8, HALF), 1)
    sub = lax.broadcasted_iota(jnp.int32, (8, HALF), 0)
    across, down = [], []
    for at in (0, 256):
        picked = [jnp.where(lane == sub + p * 8, g_ref[at + p * 8:at + p * 8 + 8, :], 0.0) for p in range(16)]
        down.append([lax.rsqrt(splat(jnp.sum(t, axis=1, keepdims=True))) for t in picked])
        while len(picked) > 1:
            picked = [picked[i] + picked[i + 1] for i in range(0, len(picked), 2)]
        across.append(splat(jnp.sum(picked[0], axis=0, keepdims=True)))
    scaled = [lax.rsqrt(v) for v in across]
    back = [jnp.sqrt(v * scale) for v in across]

    def emit(first):
        def put(at, diagonal, values):
            for k, v in enumerate(values):
                v = v * back[first + k][0:1, :]
                if k == 0:
                    v = jnp.where(lane[0:1, :] >= diagonal, v, 0.0)
                f_out[at:at + 1, (first + k) * HALF:(first + k + 1) * HALF] = v
        return put

    for p in range(16):
        at = p * 8
        a0[at:at + 8, :] = g_ref[at:at + 8, :] * (down[0][p] * scaled[0])
        a1[at:at + 8, :] = g_ref[128 + at:128 + at + 8, :] * (down[0][p] * scaled[1])
    f_out[128:256, 0:128] = jnp.zeros((128, 128), F32)
    factor_block([a0, a1], spread, 0, emit(0))
    corner = f_out[0:128, 128:256]
    less = lax.dot_general(
        corner, corner, (((0,), (0,)), ((), ())), precision=lax.Precision.HIGHEST, preferred_element_type=F32
    )
    for p in range(16):
        at = p * 8
        left = g_ref[256 + at:256 + at + 8, :] - less[at:at + 8, :] * (1.0 / scale)
        a0[at:at + 8, :] = left * (down[1][p] * scaled[1])
    factor_block([a0], spread, 128, emit(1))
    cp.wait()


def body(slab, buckets, signs, counts):
    owners = lax.axis_size("rows")
    capacity = slab.shape[1] // owners
    width = slab.shape[2]
    vm = pl.BlockSpec(memory_space=pltpu.VMEM)
    hbm = pl.BlockSpec(memory_space=pltpu.HBM)
    dma = pltpu.SemaphoreType.DMA
    sketch, gram = pl.pallas_call(
        gram_kernel,
        out_shape=(jax.ShapeDtypeStruct((BPO, width), F32), jax.ShapeDtypeStruct((384, 128), F32)),
        in_specs=[hbm] * 4,
        out_specs=(hbm, vm),
        scratch_shapes=[
            pltpu.VMEM((4, 2, 4, 2, 8, 256), F32),
            pltpu.VMEM((1, 512), jnp.int32),
            pltpu.VMEM((1, 512), jnp.int32),
            pltpu.VMEM((1, 128), jnp.int32),
            pltpu.VMEM((256, 256), F32),
            pltpu.VMEM((8, 128), jnp.int32),
            pltpu.VMEM((8, 2, 4, 8, 128), F32),
            pltpu.VMEM((8, 2, 4, 8, 128), F32),
            pltpu.VMEM((8, 8, 8, 128), F32),
            pltpu.VMEM((8, 8, 8, 128), F32),
            pltpu.VMEM((8, 128), jnp.int32),
            pltpu.VMEM((2, 8, 8, 128), jnp.int32),
            pltpu.VMEM((128, 128), jnp.int32),
            pltpu.VMEM((384, 128), F32),
            pltpu.VMEM((8, 48, 128), F32),
            pltpu.VMEM((48, 128), F32),
            pltpu.VMEM((8, 8, 128), F32),
            pltpu.VMEM((8, 128), F32),
            pltpu.VMEM((8, 8, 128), F32),
            pltpu.VMEM((48, 128), F32),
            pltpu.VMEM((384, 128), F32),
            dma((13,)),
            dma((16,)), dma((16,)), dma((16,)), dma((16,)), dma((8,)), dma((8,)),
            dma((16,)), dma((16,)), dma((16,)), dma((16,)), dma((16,)), dma((16,)),
            dma((8,)), dma((8,)), dma((8,)), dma((8,)), dma((8,)), dma((8,)),
            dma((8,)), dma((8,)), dma((8,)), dma((8,)),
        ],
        compiler_params=pltpu.CompilerParams(
            collective_id=0, has_side_effects=True, vmem_limit_bytes=60 * 1024 * 1024
        ),
    )(slab.reshape(4, 2, 4, 2, 8, width), buckets, signs, counts)
    slots = float(lax.axis_size("grp") * owners * owners * capacity)
    factor, sketch = pl.pallas_call(
        lambda *refs: factor_kernel(1.0 / slots, *refs),
        out_shape=(jax.ShapeDtypeStruct((width, width), F32), jax.ShapeDtypeStruct((BPO, width), F32)),
        in_specs=[vm, hbm],
        out_specs=(vm, hbm),
        scratch_shapes=[
            pltpu.VMEM((HALF, HALF), F32),
            pltpu.VMEM((HALF, HALF), F32),
            pltpu.VMEM((HALF, HALF), F32),
            pltpu.SemaphoreType.DMA,
        ],
        compiler_params=pltpu.CompilerParams(vmem_limit_bytes=60 * 1024 * 1024),
    )(gram, sketch)
    return (sketch.reshape(1, BPO, width), factor)


def solution(mesh):
    in_specs = (P("grp", "rows", None), P("grp", "rows"), P("grp", "rows"), P("grp", "rows"))
    out_specs = (P("grp", "rows", None), P())
    return jax.shard_map(body, mesh=mesh, in_specs=in_specs, out_specs=out_specs, check_vma=False)
```
